32 devices in a mesh: groups: 1, tensor: 16 (over z, y, core), adapter: 2 (over x).
Axes of the slice: x: 2, y: 2, z: 4, core: 2. Of those that a mesh axis runs over, the one named last changes fastest.
Arguments:
- hidden_input: bfloat16 [4096, 8192], P(('groups', 'tensor'), 'adapter'), may hold values from -6 to 6
- value_matrix: bfloat16 [8192, 1024], P('adapter', 'tensor'), may hold values from -0.0625 to 0.0625
- adapter_down_weight: bfloat16 [16, 8192, 16], P('tensor', 'adapter'), may hold values from -0.0625 to 0.0625
- adapter_up_weight: bfloat16 [16, 16, 1024], P('tensor'), may hold values from -1.5 to 1.5
- adapter_per_block: int32 [32], P(('groups', 'tensor')), may hold values from 0 to 15
- live_block_rows: int32 [32], P(('groups', 'tensor')), may hold values from 1 to 128
Outputs:
- values_out: bfloat16 [4096, 1024], P(('groups', 'tensor'), 'adapter')
The draws below stay inside these ranges and needn't reach their ends.
All inputs are finite; a program needn't handle non-finite values.
Results may differ from the reference program's by a relative error of at most 0.0038.
Values may be sent and summed in bfloat16 or wider, within the bound.
No kernel may reach another device: no remote copies, remote signals or barrier semaphores. Data moves between devices by JAX's collectives and lax.ppermute only.
A program may use at most 64 MiB of HBM per device.

```python
import math
import jax
import jax.numpy as jnp
import numpy as np
from jax import lax

MODEL_WIDTH = 8192
ADAPTER_RANK = 16
BLK = 128
VALUE_WIDTH = 1024
ADAPTER_COUNT = 16
TOKENS = 4096
NBLK = 32


def touch_ends(entries, own_key, least, largest):
    spot = [jax.random.randint(jax.random.fold_in(own_key, axis), (), 0, length) for axis, length in enumerate(entries.shape)]
    main_axis = entries.shape.index(max(entries.shape))
    neighbour = spot[:main_axis] + [(spot[main_axis] + 1) % entries.shape[main_axis]] + spot[main_axis + 1:]
    return entries.at[tuple(spot)].set(least).at[tuple(neighbour)].set(largest)


def levels(stream_key, shape, cuts, smallest, largest):
    def one(axis_at, shards_of):
        steps = jax.random.uniform(jax.random.fold_in(jax.random.fold_in(stream_key, 6), axis_at), (shards_of,), jnp.float32, smallest / len(cuts), largest / len(cuts))
        return jnp.repeat(jnp.exp(steps), shape[axis_at] // shards_of).reshape((-1,) + (1,) * (len(shape) - axis_at - 1))

    loudness = one(*cuts[0])
    for cut in cuts[1:]:
        loudness = loudness * one(*cut)
    return loudness


def cumulative_ranks(amount, slope):
    portions = [(1 << 20) // math.isqrt(grade ** slope) + 1 for grade in range(1, amount + 1)]
    deviation = 1 + sum(portions) // (1 << 30)
    return np.cumsum(np.array([max(1, weight // deviation) for weight in portions]))


def skewed_ids(rng, shape, amount, lean):
    listing = cumulative_ranks(amount, lean)
    pick = jax.random.randint(jax.random.fold_in(rng, 1), shape, 0, int(listing[amount - 1]))
    standing = jnp.searchsorted(jnp.asarray(listing, jnp.int32), pick, side="right")
    return jax.random.permutation(jax.random.fold_in(rng, 2), amount)[standing].astype(jnp.int32)


def normal_values(rng, shape, width, limit, shards=(), held_as=jnp.bfloat16):
    gain = levels(rng, shape, shards, -0.22, 0.18) if shards else 1.0
    values = jax.random.normal(rng, shape, jnp.float32) * width * gain
    return jnp.minimum(jnp.maximum(values, -limit), limit).astype(held_as)


def setup_inputs(seed: int = 0, part: int = 0) -> dict:
    key_of = jax.random.split(jax.random.key(seed), 7)
    part_keys = jax.random.split(jax.random.fold_in(key_of[6], part), 7)
    return {
        "hidden_input": normal_values(part_keys[0], (TOKENS, MODEL_WIDTH), 1.0, 6.0, ((0, 16), (1, 2))),
        "value_matrix": normal_values(key_of[1], (MODEL_WIDTH, VALUE_WIDTH), MODEL_WIDTH ** -0.5, 0.0625, ((0, 2), (1, 16))),
        "adapter_down_weight": normal_values(key_of[2], (ADAPTER_COUNT, MODEL_WIDTH, ADAPTER_RANK), MODEL_WIDTH ** -0.5, 0.0625, ((0, 16), (1, 2))),
        "adapter_up_weight": normal_values(key_of[3], (ADAPTER_COUNT, ADAPTER_RANK, VALUE_WIDTH), ADAPTER_RANK ** -0.5, 1.5, ((0, 16),)),
        "adapter_per_block": touch_ends(skewed_ids(part_keys[4], (NBLK,), ADAPTER_COUNT, 2), jax.random.fold_in(part_keys[4], 3), 0, ADAPTER_COUNT - 1).astype(jnp.int32),
        "live_block_rows": touch_ends(jax.random.randint(part_keys[5], (NBLK,), 1, BLK + 1), jax.random.fold_in(part_keys[5], 1), 1, BLK).astype(jnp.int32),
    }


def reference(hidden_input, value_matrix, adapter_down_weight, adapter_up_weight, adapter_per_block, live_block_rows):
    blocks = hidden_input.reshape(NBLK, BLK, MODEL_WIDTH)

    def per_block(operands):
        tok_block, adapter_number, live_rows = operands
        base_out = jnp.dot(tok_block, value_matrix, preferred_element_type=jnp.float32)
        down_product = lax.dynamic_index_in_dim(adapter_down_weight, adapter_number.astype(jnp.int32), 0, keepdims=False)
        shrink = jnp.dot(tok_block, down_product, preferred_element_type=jnp.float32)
        live_mask = jnp.arange(BLK, dtype=jnp.int32)[:, None] < live_rows
        shrink = jnp.where(live_mask, shrink, jnp.zeros_like(shrink)).astype(jnp.bfloat16)
        up_product = lax.dynamic_index_in_dim(adapter_up_weight, adapter_number.astype(jnp.int32), 0, keepdims=False)
        low_rank = jnp.dot(shrink, up_product, preferred_element_type=jnp.float32)
        return (base_out + low_rank).astype(jnp.bfloat16)

    result = lax.map(per_block, (blocks, adapter_per_block, live_block_rows))
    return result.reshape(TOKENS, VALUE_WIDTH)
```

```python
import jax
import jax.numpy as jnp
from jax import lax
from jax.sharding import PartitionSpec as P

BLK = 128
F32 = jnp.float32
BF16 = jnp.bfloat16


def dot_nt(a, b):
    return lax.dot_general(a, b, (((1,), (1,)), ((), ())), preferred_element_type=F32)


def make_body(tensor, adapters):
    depth = tensor // 4
    low = depth // adapters

    def over_tensor(array, flip):
        return lax.ppermute(array, "tensor", perm=[(i, i ^ flip) for i in range(tensor)])

    def over_adapter(array, flip):
        return lax.ppermute(array, "adapter", perm=[(i, i ^ flip) for i in range(adapters)])

    def over_both(array, flip_t, flip_a):
        pairs = [
            (i * adapters + j, (i ^ flip_t) * adapters + (j ^ flip_a))
            for i in range(tensor)
            for j in range(adapters)
        ]
        return lax.ppermute(array, ("tensor", "adapter"), perm=pairs)

    def body(hidden, value, down, up, chosen, live):
        t, x = lax.axis_index("tensor"), lax.axis_index("adapter")
        z, y, core = t // 4, (t // 2) % 2, t % 2
        rows, features = hidden.shape
        width = value.shape[1]
        homes, rank, wide = up.shape
        blocks = rows // BLK
        first = (blocks // 2) * BLK

        theirs = [over_tensor(hidden[:first], 2), over_tensor(hidden[first:], 2)]
        packet = jnp.concatenate([value.T, down.transpose(0, 2, 1).reshape(homes * rank, features)])
        units = {0: packet}
        bit = depth // 2
        while bit:
            units.update({a ^ bit: over_tensor(u, 4 * bit) for a, u in units.items()})
            bit //= 2
        pairs = {a: (u, over_tensor(u, 1)) for a, u in units.items()}

        ids = jnp.stack([chosen, live])
        ids = jnp.concatenate([ids, over_tensor(ids, 2)], axis=1)
        ups = lax.dynamic_slice_in_dim(up, x * (wide // adapters), wide // adapters, 2)[None]
        bit = 1
        while bit < tensor:
            ups = jnp.concatenate([ups, over_tensor(ups, bit)])
            bit *= 2

        w_all = jnp.concatenate([u[:width] for a in range(depth) for u in pairs[a]])
        d_all = jnp.concatenate([u[width:] for a in range(depth) for u in pairs[a]])

        relative = (ids[0] // homes) ^ t
        here = (relative & 2) == 0
        slot = (relative // 4) * 2 + relative % 2
        which = slot * homes + ids[0] % homes

        ups = ups.reshape(tensor, homes, rank, low, 2, 2, width)
        ups = lax.dynamic_index_in_dim(ups, y, 4, keepdims=False)
        z_low = z % low
        order = [
            lax.dynamic_index_in_dim(ups, z_low ^ a, 3, keepdims=False) for a in range(low)
        ]
        ups = jnp.stack(order, axis=3)
        ups = jnp.where(core == 1, ups[..., ::-1, :], ups)
        ups = ups.reshape(tensor * homes, rank, low * 2 * width)
        up_index = relative * homes + ids[0] % homes

        mine_part = (z // low) ^ x

        def work(x_rows, b0):
            count = x_rows.shape[0] // BLK
            base = dot_nt(x_rows, w_all).reshape(-1, adapters, low * 2 * width)
            kept = lax.dynamic_index_in_dim(base, mine_part, 1, keepdims=False)
            sent = [
                lax.dynamic_index_in_dim(base, mine_part ^ k, 1, keepdims=False)
                for k in range(1, adapters)
            ]
            for k in range(1, adapters):
                kept = kept + over_adapter(sent[k - 1], k)
            shrink = dot_nt(x_rows, d_all).reshape(count, BLK, -1, rank)
            spots = jnp.arange(shrink.shape[2], dtype=jnp.int32)
            hot = (which[b0 : b0 + count, None] == spots) & here[b0 : b0 + count, None]
            alive = jnp.arange(BLK, dtype=jnp.int32) < ids[1, b0 : b0 + count, None]
            mask = hot[:, None, :, None] & alive[:, :, None, None]
            shrink = jnp.where(mask, shrink, 0.0).sum(axis=2)
            return kept, shrink

        def finish(kept, shrink, b0):
            count = shrink.shape[0]
            mid = shrink.astype(BF16)
            picked = jnp.stack(
                [
                    lax.dynamic_index_in_dim(ups, up_index[b], 0, keepdims=False)
                    for b in range(b0, b0 + count)
                ]
            )
            extra = jnp.einsum("bir,brv->biv", mid, picked, preferred_element_type=F32)
            return (kept + extra.reshape(kept.shape)).astype(BF16)

        half = blocks // 2
        kept_own, m_own = work(hidden, 0)
        kept_a, m_a = work(theirs[0], blocks)
        kept_b, m_b = work(theirs[1], blocks + half)
        m = jnp.concatenate([m_own, m_a, m_b])
        for k in range(1, adapters):
            m = m + over_adapter(m, k)
        swapped = over_tensor(m.astype(BF16), 2)
        swapped = jnp.concatenate([swapped[blocks:], swapped[:blocks]])
        m = m.astype(BF16) + swapped

        out_a = over_tensor(finish(kept_a, m[blocks : blocks + half], blocks), 2)
        out_b = over_tensor(finish(kept_b, m[blocks + half :], blocks + half), 2)
        out_own = finish(kept_own, m[:blocks], 0)
        pair = jnp.stack([out_own, jnp.concatenate([out_a, out_b])], axis=1)
        pair = pair.reshape(rows, 2, low, 2, width)
        pair = jnp.where(y == 1, pair[:, ::-1], pair)
        pair = jnp.where(core == 1, pair[:, :, :, ::-1], pair)
        pair = jnp.stack(
            [lax.dynamic_index_in_dim(pair, z_low ^ a, 2, keepdims=False) for a in range(low)],
            axis=1,
        )
        return pair.reshape(rows, wide // adapters)

    return body


def solution(mesh):
    in_specs = (
        P(("groups", "tensor"), "adapter"),
        P("adapter", "tensor"),
        P("tensor", "adapter", None),
        P("tensor", None, None),
        P(("groups", "tensor")),
        P(("groups", "tensor")),
    )
    out_specs = P(("groups", "tensor"), "adapter")
    body = make_body(mesh.shape["tensor"], mesh.shape["adapter"])
    return jax.shard_map(body, mesh=mesh, in_specs=in_specs, out_specs=out_specs, check_vma=False)
```

```python
import functools

import jax
import jax.numpy as jnp
from jax import lax
from jax.experimental import pallas as pl
from jax.experimental.pallas import tpu as pltpu
from jax.sharding import PartitionSpec as P

BLK = 128
LANES = 128
F32 = jnp.float32
BF16 = jnp.bfloat16
MIB = 1 << 20


def dot_nt(a, b):
    return lax.dot_general(a, b, (((1,), (1,)), ((), ())), preferred_element_type=F32)


def swaps(tensor, adapters):
    def over_tensor(array, flip):
        return lax.ppermute(array, "tensor", perm=[(i, i ^ flip) for i in range(tensor)])

    def over_adapter(array, flip):
        return lax.ppermute(array, "adapter", perm=[(i, i ^ flip) for i in range(adapters)])

    return over_tensor, over_adapter


def make_general_body(tensor, adapters):
    depth = tensor // 4
    low = depth // adapters
    over_tensor, over_adapter = swaps(tensor, adapters)

    def body(hidden, value, down, up, chosen, live):
        t, x = lax.axis_index("tensor"), lax.axis_index("adapter")
        z, y, core = t // 4, (t // 2) % 2, t % 2
        rows, features = hidden.shape
        width = value.shape[1]
        homes, rank, wide = up.shape
        blocks = rows // BLK

        theirs = over_tensor(hidden, 2)
        packet = jnp.concatenate([value.T, down.transpose(0, 2, 1).reshape(homes * rank, features)])
        units = {0: packet}
        bit = depth // 2
        while bit:
            units.update({a ^ bit: over_tensor(u, 4 * bit) for a, u in units.items()})
            bit //= 2
        pairs = {a: (u, over_tensor(u, 1)) for a, u in units.items()}

        ids = jnp.stack([chosen, live])
        ids = jnp.concatenate([ids, over_tensor(ids, 2)], axis=1)
        ups = lax.dynamic_slice_in_dim(up, x * (wide // adapters), wide // adapters, 2)[None]
        bit = 1
        while bit < tensor:
            ups = jnp.concatenate([ups, over_tensor(ups, bit)])
            bit *= 2

        w_all = jnp.concatenate([u[:width] for a in range(depth) for u in pairs[a]])
        d_all = jnp.concatenate([u[width:] for a in range(depth) for u in pairs[a]])

        relative = (ids[0] // homes) ^ t
        here = (relative & 2) == 0
        slot = (relative // 4) * 2 + relative % 2
        which = slot * homes + ids[0] % homes

        ups = ups.reshape(tensor, homes, rank, low, 2, 2, width)
        ups = lax.dynamic_index_in_dim(ups, y, 4, keepdims=False)
        z_low = z % low
        order = [lax.dynamic_index_in_dim(ups, z_low ^ a, 3, keepdims=False) for a in range(low)]
        ups = jnp.stack(order, axis=3)
        ups = jnp.where(core == 1, ups[..., ::-1, :], ups)
        ups = ups.reshape(tensor * homes, rank, low * 2 * width)
        up_index = relative * homes + ids[0] % homes

        part = (z // low) ^ x

        def work(x_rows, b0):
            count = x_rows.shape[0] // BLK
            base = dot_nt(x_rows, w_all).reshape(-1, adapters, low * 2 * width)
            kept = lax.dynamic_index_in_dim(base, part, 1, keepdims=False)
            for k in range(1, adapters):
                sent = lax.dynamic_index_in_dim(base, part ^ k, 1, keepdims=False)
                kept = kept + over_adapter(sent, k)
            shrink = dot_nt(x_rows, d_all).reshape(count, BLK, -1, rank)
            spots = jnp.arange(shrink.shape[2], dtype=jnp.int32)
            hot = (which[b0 : b0 + count, None] == spots) & here[b0 : b0 + count, None]
            alive = jnp.arange(BLK, dtype=jnp.int32) < ids[1, b0 : b0 + count, None]
            mask = hot[:, None, :, None] & alive[:, :, None, None]
            return kept, jnp.where(mask, shrink, 0.0).sum(axis=2)

        def finish(kept, shrink, b0):
            mid = shrink.astype(BF16)
            picked = [
                lax.dynamic_index_in_dim(ups, up_index[b], 0, keepdims=False)
                for b in range(b0, b0 + shrink.shape[0])
            ]
            extra = jnp.einsum("bir,brv->biv", mid, jnp.stack(picked), preferred_element_type=F32)
            return (kept + extra.reshape(kept.shape)).astype(BF16)

        kept_own, m_own = work(hidden, 0)
        kept_their, m_their = work(theirs, blocks)
        m = jnp.concatenate([m_own, m_their])
        total = m
        for k in range(1, adapters):
            total = total + over_adapter(m, k)
        m = total.astype(BF16)
        swapped = over_tensor(m, 2)
        m = m + jnp.concatenate([swapped[blocks:], swapped[:blocks]])
        out_their = over_tensor(finish(kept_their, m[blocks:], blocks), 2)
        out_own = finish(kept_own, m[:blocks], 0)
        pair = jnp.stack([out_own, out_their], axis=1)
        pair = pair.reshape(rows, 2, low, 2, width)
        pair = jnp.where(y == 1, pair[:, ::-1], pair)
        pair = jnp.where(core == 1, pair[:, :, :, ::-1], pair)
        pair = jnp.stack(
            [lax.dynamic_index_in_dim(pair, z_low ^ a, 2, keepdims=False) for a in range(low)],
            axis=1,
        )
        return pair.reshape(rows, wide // adapters)

    return body


RANK = 16
WIDTH = 64
DEPTH = 4
TILE = 2 * WIDTH
HALF = 2 * TILE
UP_TILES = 4


def place():
    t = lax.axis_index("tensor")
    z, y, core = t // 4, (t // 2) % 2, t % 2
    part = (z // 2) ^ lax.axis_index("adapter")
    return t, z % 2, y, core, part


def prep_kernel(chosen, live, value, down, up, packet, ids):
    x = lax.axis_index("adapter")
    features = value.shape[1]
    packet[:WIDTH, :features] = value[...]
    packet[pl.ds(WIDTH, RANK), :features] = down[...]
    packet[pl.ds(WIDTH, RANK), pl.ds(features, LANES)] = jnp.zeros((RANK, LANES), BF16)
    for j in range(UP_TILES):
        start = pl.multiple_of((x * UP_TILES + j) * LANES, LANES)
        packet[pl.ds(j * RANK, RANK), pl.ds(features, LANES)] = up[:, pl.ds(start, LANES)]
    lane = lax.broadcasted_iota(jnp.int32, ids.shape, 1)
    line = jnp.zeros(ids.shape, jnp.int32)
    for b in range(2):
        line = jnp.where(lane == b, chosen[b], line)
        line = jnp.where(lane == 2 + b, live[b], line)
    ids[...] = line


def prep(chosen, live, value, down, up):
    features = value.shape[1]
    vmem, smem = pl.BlockSpec(memory_space=pltpu.VMEM), pl.BlockSpec(memory_space=pltpu.SMEM)
    return pl.pallas_call(
        prep_kernel,
        out_shape=[
            jax.ShapeDtypeStruct((WIDTH + RANK, features + LANES), BF16),
            jax.ShapeDtypeStruct((8, LANES), jnp.int32),
        ],
        in_specs=[smem] * 2 + [vmem] * 3,
        out_specs=[vmem] * 2,
    )(chosen, live, value, down, up)


def compute_kernel(chosen, live, ids_p, mine, theirs, *refs):
    units, (kept, to_x, to_y, to_xy, up_own, w, d) = refs[: 2 * DEPTH], refs[2 * DEPTH :]
    t, _, _, core, part = place()
    rows, features = mine.shape
    for a in range(DEPTH):
        base = ((a // 2) ^ part) * HALF + (a % 2) * TILE
        for k in range(2):
            start = pl.multiple_of(base + (core ^ k) * WIDTH, WIDTH)
            w[pl.ds(start, WIDTH), :] = units[2 * a + k][:WIDTH, :features]
    up_own[...] = jnp.zeros_like(up_own)
    to_y[pl.ds(rows + RANK, WIDTH), :] = jnp.zeros((WIDTH, HALF), F32)
    for b in range(4):
        relative = (chosen[b] if b < 2 else ids_p[0, b - 2]) ^ t
        spot = (relative // 4) * 2 + relative % 2
        here = ((relative // 2) % 2) == 0
        lanes = pl.ds(b % 2 * LANES, LANES)
        d[b] = jnp.zeros_like(d[b])
        for u in range(2 * DEPTH):

            @pl.when(here & (spot == u))
            def _():
                d[b] = units[u][pl.ds(WIDTH, RANK), :features]
                up = units[u][:WIDTH, pl.ds(features, LANES)].astype(F32)
                if b < 2:
                    up_own[:, lanes] = up
                else:
                    to_y[pl.ds(rows + RANK, WIDTH), lanes] = up

    w_kept, w_sent = w[pl.ds(0, HALF), :], w[pl.ds(HALF, HALF), :]
    kept[:rows, :] = dot_nt(mine[...], w_kept)
    to_x[:rows, :] = dot_nt(mine[...], w_sent)
    to_y[:rows, :] = dot_nt(theirs[...], w_kept)
    to_xy[:rows, :] = dot_nt(theirs[...], w_sent)
    line = pl.ds(rows, RANK)
    for b in range(4):
        at = pl.ds(b % 2 * BLK, BLK)
        m = dot_nt(d[b], (mine if b < 2 else theirs)[at, :])
        limit = live[b] if b < 2 else ids_p[0, b]
        m = jnp.where(lax.broadcasted_iota(jnp.int32, m.shape, 1) < limit, m, 0.0)
        if b < 2:
            kept[line, at] = m
            to_x[line, at] = m
        else:
            to_y[line, at] = m
            to_xy[line, at] = m


def compute(scalars, rows, units):
    count, features = rows[0].shape
    vmem, smem = pl.BlockSpec(memory_space=pltpu.VMEM), pl.BlockSpec(memory_space=pltpu.SMEM)
    short = jax.ShapeDtypeStruct((count + RANK, HALF), F32)
    long = jax.ShapeDtypeStruct((count + RANK + WIDTH, HALF), F32)
    return pl.pallas_call(
        compute_kernel,
        out_shape=[short, short, long, short, jax.ShapeDtypeStruct((WIDTH, HALF), F32)],
        in_specs=[smem] * 3 + [vmem] * (2 + len(units)),
        out_specs=[vmem] * 5,
        scratch_shapes=[
            pltpu.VMEM((2 * HALF, features), BF16),
            pltpu.VMEM((4, RANK, features), BF16),
        ],
        compiler_params=pltpu.CompilerParams(vmem_limit_bytes=48 * MIB),
        cost_estimate=pl.CostEstimate(
            flops=4 * count * features * 2 * HALF, bytes_accessed=10 * MIB, transcendentals=0
        ),
    )(*scalars, *rows, *units)


def final_kernel(kept, up_own, from_x, from_y, from_xy, out):
    _, z_low, y, _, _ = place()
    rows = out.shape[0]
    line = pl.ds(rows, RANK)
    m = (kept[line, :] + from_x[line, :]) + (from_y[line, :] + from_xy[line, :])
    mid = m.T.astype(BF16)
    up = (up_own[...] + from_y[pl.ds(rows + RANK, WIDTH), :]).astype(BF16)
    for tile in range(2):
        cols = pl.ds(tile * LANES, LANES)
        for side in range(2):
            j = 2 * (z_low ^ tile) + (y ^ side)
            lanes = pl.ds(pl.multiple_of(j * LANES, LANES), LANES)
            for b in range(2):
                span = pl.ds(b * BLK, BLK)
                if side == 0:
                    base = kept[span, cols] + from_x[span, cols]
                else:
                    base = from_y[span, cols] + from_xy[span, cols]
                picked = jnp.zeros((RANK, LANES), BF16)
                for i in range(UP_TILES):
                    piece = up[i * RANK : (i + 1) * RANK, b * LANES : (b + 1) * LANES]
                    picked = jnp.where(j == i, piece, picked)
                extra = jnp.dot(
                    mid[b * BLK : (b + 1) * BLK], picked, preferred_element_type=F32
                )
                out[span, lanes] = (base + extra).astype(BF16)


def final(rows, *args):
    vmem = pl.BlockSpec(memory_space=pltpu.VMEM)
    return pl.pallas_call(
        final_kernel,
        out_shape=jax.ShapeDtypeStruct((rows, 2 * HALF), BF16),
        in_specs=[vmem] * len(args),
        out_specs=vmem,
    )(*args)


def make_body(tensor, adapters):
    over_tensor, over_adapter = swaps(tensor, adapters)
    tie = lax.optimization_barrier

    def over_both(array):
        pairs = [
            (i * adapters + j, (i ^ 2) * adapters + (j ^ 1))
            for i in range(tensor)
            for j in range(adapters)
        ]
        return lax.ppermute(array, ("tensor", "adapter"), perm=pairs)

    def body(hidden, value, down, up, chosen, live):
        rows, features = hidden.shape
        theirs = over_tensor(hidden, 2)
        packet, ids = prep(
            chosen, live, value.T, down.transpose(0, 2, 1).reshape(RANK, features), up[0]
        )
        ids_p = over_tensor(ids, 2)
        u2 = over_tensor(packet, 8)
        u1 = over_tensor(packet, 4)
        v0 = over_tensor(packet, 1)
        u2, u1, v0 = tie((u2, u1, v0))
        u3 = over_tensor(u2, 4)
        v2, v1 = over_tensor(u2, 1), over_tensor(u1, 1)
        v3 = over_tensor(u3, 1)
        units = (packet, v0, u1, v1, u2, v2, u3, v3)
        kept, to_x, to_y, to_xy, up_own = compute((chosen, live, ids_p), (hidden, theirs), units)
        from_xy = over_both(to_xy)
        from_x = over_adapter(to_x, 1)
        from_y = over_tensor(to_y, 2)
        return final(rows, kept, up_own, from_x, from_y, from_xy)

    return body


def solution(mesh):
    in_specs = (
        P(("groups", "tensor"), "adapter"),
        P("adapter", "tensor"),
        P("tensor", "adapter", None),
        P("tensor", None, None),
        P(("groups", "tensor")),
        P(("groups", "tensor")),
    )
    out_specs = P(("groups", "tensor"), "adapter")
    tensor, adapters = mesh.shape["tensor"], mesh.shape["adapter"]

    def run(hidden, value, down, up, chosen, live):
        blocks = chosen.shape[0] // (mesh.shape["groups"] * tensor)
        fits = (tensor, adapters, blocks) == (4 * DEPTH, 2, 2)
        fits = fits and up.shape == (tensor, RANK, tensor * WIDTH)
        make = make_body if fits else make_general_body
        body = make(tensor, adapters)
        mapped = jax.shard_map(
            body, mesh=mesh, in_specs=in_specs, out_specs=out_specs, check_vma=False
        )
        return mapped(hidden, value, down, up, chosen, live)

    return run
```

```python
import jax
import jax.numpy as jnp
from jax import lax
from jax.experimental import pallas as pl
from jax.experimental.pallas import tpu as pltpu
from jax.sharding import PartitionSpec as P

BLK = 128
LANES = 128
F32 = jnp.float32
BF16 = jnp.bfloat16
MIB = 1 << 20


def dot_nt(a, b):
    return lax.dot_general(a, b, (((1,), (1,)), ((), ())), preferred_element_type=F32)


def swaps(tensor, adapters):
    def over_tensor(array, flip):
        return lax.ppermute(array, "tensor", perm=[(i, i ^ flip) for i in range(tensor)])

    def over_adapter(array, flip):
        return lax.ppermute(array, "adapter", perm=[(i, i ^ flip) for i in range(adapters)])

    return over_tensor, over_adapter


def make_general_body(tensor, adapters):
    depth = tensor // 4
    low = depth // adapters
    over_tensor, over_adapter = swaps(tensor, adapters)

    def body(hidden, value, down, up, chosen, live):
        t, x = lax.axis_index("tensor"), lax.axis_index("adapter")
        z, y, core = t // 4, (t // 2) % 2, t % 2
        rows, features = hidden.shape
        width = value.shape[1]
        homes, rank, wide = up.shape
        blocks = rows // BLK

        theirs = over_tensor(hidden, 2)
        packet = jnp.concatenate([value.T, down.transpose(0, 2, 1).reshape(homes * rank, features)])
        units = {0: packet}
        bit = depth // 2
        while bit:
            units.update({a ^ bit: over_tensor(u, 4 * bit) for a, u in units.items()})
            bit //= 2
        pairs = {a: (u, over_tensor(u, 1)) for a, u in units.items()}

        ids = jnp.stack([chosen, live])
        ids = jnp.concatenate([ids, over_tensor(ids, 2)], axis=1)
        ups = lax.dynamic_slice_in_dim(up, x * (wide // adapters), wide // adapters, 2)[None]
        bit = 1
        while bit < tensor:
            ups = jnp.concatenate([ups, over_tensor(ups, bit)])
            bit *= 2

        w_all = jnp.concatenate([u[:width] for a in range(depth) for u in pairs[a]])
        d_all = jnp.concatenate([u[width:] for a in range(depth) for u in pairs[a]])

        relative = (ids[0] // homes) ^ t
        here = (relative & 2) == 0
        slot = (relative // 4) * 2 + relative % 2
        which = slot * homes + ids[0] % homes

        ups = ups.reshape(tensor, homes, rank, low, 2, 2, width)
        ups = lax.dynamic_index_in_dim(ups, y, 4, keepdims=False)
        z_low = z % low
        order = [lax.dynamic_index_in_dim(ups, z_low ^ a, 3, keepdims=False) for a in range(low)]
        ups = jnp.stack(order, axis=3)
        ups = jnp.where(core == 1, ups[..., ::-1, :], ups)
        ups = ups.reshape(tensor * homes, rank, low * 2 * width)
        up_index = relative * homes + ids[0] % homes

        part = (z // low) ^ x

        def work(x_rows, b0):
            count = x_rows.shape[0] // BLK
            base = dot_nt(x_rows, w_all).reshape(-1, adapters, low * 2 * width)
            kept = lax.dynamic_index_in_dim(base, part, 1, keepdims=False)
            for k in range(1, adapters):
                sent = lax.dynamic_index_in_dim(base, part ^ k, 1, keepdims=False)
                kept = kept + over_adapter(sent, k)
            shrink = dot_nt(x_rows, d_all).reshape(count, BLK, -1, rank)
            spots = jnp.arange(shrink.shape[2], dtype=jnp.int32)
            hot = (which[b0 : b0 + count, None] == spots) & here[b0 : b0 + count, None]
            alive = jnp.arange(BLK, dtype=jnp.int32) < ids[1, b0 : b0 + count, None]
            mask = hot[:, None, :, None] & alive[:, :, None, None]
            return kept, jnp.where(mask, shrink, 0.0).sum(axis=2)

        def finish(kept, shrink, b0):
            mid = shrink.astype(BF16)
            picked = [
                lax.dynamic_index_in_dim(ups, up_index[b], 0, keepdims=False)
                for b in range(b0, b0 + shrink.shape[0])
            ]
            extra = jnp.einsum("bir,brv->biv", mid, jnp.stack(picked), preferred_element_type=F32)
            return (kept + extra.reshape(kept.shape)).astype(BF16)

        kept_own, m_own = work(hidden, 0)
        kept_their, m_their = work(theirs, blocks)
        m = jnp.concatenate([m_own, m_their])
        total = m
        for k in range(1, adapters):
            total = total + over_adapter(m, k)
        m = total.astype(BF16)
        swapped = over_tensor(m, 2)
        m = m + jnp.concatenate([swapped[blocks:], swapped[:blocks]])
        out_their = over_tensor(finish(kept_their, m[blocks:], blocks), 2)
        out_own = finish(kept_own, m[:blocks], 0)
        pair = jnp.stack([out_own, out_their], axis=1)
        pair = pair.reshape(rows, 2, low, 2, width)
        pair = jnp.where(y == 1, pair[:, ::-1], pair)
        pair = jnp.where(core == 1, pair[:, :, :, ::-1], pair)
        pair = jnp.stack(
            [lax.dynamic_index_in_dim(pair, z_low ^ a, 2, keepdims=False) for a in range(low)],
            axis=1,
        )
        return pair.reshape(rows, wide // adapters)

    return body


RANK = 16
WIDTH = 64
DEPTH = 4
TILE = 2 * WIDTH
HALF = 2 * TILE
UP_TILES = 4
PAD = 24
VMEM = 16 * MIB
IN_SMEM = pl.BlockSpec(memory_space=pltpu.SMEM)
IN_VMEM = pl.BlockSpec(memory_space=pltpu.VMEM)
IN_HBM = pl.BlockSpec(memory_space=pltpu.HBM)
IN_ANY = pl.BlockSpec(memory_space=pl.ANY)


def place():
    t = lax.axis_index("tensor")
    z, y, core = t // 4, (t // 2) % 2, t % 2
    part = (z // 2) ^ lax.axis_index("adapter")
    return t, z % 2, y, core, part


def prep_kernel(chosen, live, down, up, packet, ids):
    x = lax.axis_index("adapter")
    features = down.shape[1]
    packet[:, :features] = down[...]
    start = pl.multiple_of(x * 2 * HALF, LANES)
    packet[:, pl.ds(features, 2 * HALF)] = up[:, pl.ds(start, 2 * HALF)]
    lane = lax.broadcasted_iota(jnp.int32, ids.shape, 1)
    line = jnp.zeros(ids.shape, jnp.int32)
    for b in range(2):
        line = jnp.where(lane == b, chosen[b], line)
        line = jnp.where(lane == 2 + b, live[b], line)
    ids[...] = line


def prep(chosen, live, down, up):
    features = down.shape[1]
    return pl.pallas_call(
        prep_kernel,
        out_shape=[
            jax.ShapeDtypeStruct((RANK, features + 2 * HALF), BF16),
            jax.ShapeDtypeStruct((8, LANES), jnp.int32),
        ],
        in_specs=[IN_SMEM] * 2 + [IN_VMEM] * 2,
        out_specs=[IN_VMEM] * 2,
        compiler_params=pltpu.CompilerParams(vmem_limit_bytes=60 * MIB),
        cost_estimate=pl.CostEstimate(flops=0, bytes_accessed=MIB, transcendentals=0),
    )(chosen, live, down, up)


def gather_wide(wide, w, sems):
    _, _, _, core, part = place()
    copies = []
    for a in range(DEPTH):
        base = ((a // 2) ^ part) * HALF + (a % 2) * TILE
        for k in range(2):
            start = pl.multiple_of(base + (core ^ k) * WIDTH, WIDTH)
            i = 2 * a + k
            copies.append(
                pltpu.make_async_copy(wide[i], w.at[pl.ds(start, WIDTH), :], sems.at[i])
            )
    for c in copies:
        c.start()
    return copies


def load_rows(pieces, rows_in, sems):
    at, copies = 0, []
    for i, ref in enumerate(pieces):
        copies.append(
            pltpu.make_async_copy(ref, rows_in.at[pl.ds(at, ref.shape[0])], sems.at[i])
        )
        at += ref.shape[0]
    for c in copies:
        c.start()
    return copies


def their_kernel(theirs, *refs):
    wide, (to_y, to_xy, w, rows_in, w_sem, r_sem) = refs[: 2 * DEPTH], refs[2 * DEPTH :]
    rows = rows_in.shape[0]
    copies = load_rows((theirs,), rows_in, r_sem) + gather_wide(wide, w, w_sem)
    for c in copies:
        c.wait()
    to_xy[:rows, :] = dot_nt(rows_in[...], w[pl.ds(HALF, HALF), :])
    to_y[:rows, :] = dot_nt(rows_in[...], w[pl.ds(0, HALF), :])
    for out in (to_y, to_xy):
        out[pl.ds(rows, PAD), :] = jnp.zeros((PAD, HALF), F32)


def their_sums(theirs, wide):
    rows, features = theirs.shape
    return pl.pallas_call(
        their_kernel,
        out_shape=[jax.ShapeDtypeStruct((rows + PAD, HALF), F32)] * 2,
        in_specs=[IN_ANY] * (1 + len(wide)),
        out_specs=[IN_VMEM] * 2,
        scratch_shapes=[
            pltpu.VMEM((2 * HALF, features), BF16),
            pltpu.VMEM((rows, features), BF16),
            pltpu.SemaphoreType.DMA((2 * DEPTH,)),
            pltpu.SemaphoreType.DMA((1,)),
        ],
        compiler_params=pltpu.CompilerParams(vmem_limit_bytes=VMEM),
        cost_estimate=pl.CostEstimate(flops=0, bytes_accessed=0, transcendentals=0),
    )(theirs, *wide)


def own_kernel(ids, ids_p, mine, theirs, narrow, narrow_v, *refs):
    wide, refs = refs[: 2 * DEPTH], refs[2 * DEPTH :]
    kept, to_x, m_y, m_xy, up_own, w, d, up, rows_in, w_sem, d_sem, r_sem = refs
    t = lax.axis_index("tensor")
    rows, features = mine.shape
    cols = pl.ds(0, features)
    copies = load_rows((mine, theirs), rows_in, r_sem) + gather_wide(wide, w, w_sem)

    def fetch(b, ref, line):
        lines = pl.ds(line, RANK)
        return [
            pltpu.make_async_copy(ref.at[lines, cols], d.at[b], d_sem.at[2 * b]),
            pltpu.make_async_copy(
                ref.at[lines, pl.ds(features, 2 * HALF)], up.at[b], d_sem.at[2 * b + 1]
            ),
        ]

    where = []
    for b in range(4):
        relative = (ids[0, b] if b < 2 else ids_p[0, b - 2]) ^ t
        here = ((relative // 2) % 2) == 0
        line, other = pl.multiple_of(relative // 4 * RANK, RANK), relative % 2
        where.append(here)

        @pl.when(jnp.logical_not(here))
        def _():
            d[b] = jnp.zeros_like(d[b])
            up[b] = jnp.zeros_like(up[b])

        for i, ref in enumerate((narrow, narrow_v)):

            @pl.when(here & (other == i))
            def _():
                for c in fetch(b, ref, line):
                    c.start()

    for c in copies:
        c.wait()
    to_x[:rows, :] = dot_nt(rows_in[pl.ds(0, rows), :], w[pl.ds(HALF, HALF), :])
    kept[:rows, :] = dot_nt(rows_in[pl.ds(0, rows), :], w[pl.ds(0, HALF), :])
    for b, here in enumerate(where):

        @pl.when(here)
        def _():
            for c in fetch(b, narrow, 0):
                c.wait()

    for b in range(4):
        at = pl.ds(b % 2 * BLK, BLK)
        m = dot_nt(d[b], rows_in[pl.ds(b * BLK, BLK), :])
        limit = ids[0, 2 + b] if b < 2 else ids_p[0, b]
        m = jnp.where(lax.broadcasted_iota(jnp.int32, m.shape, 1) < limit, m, 0.0)
        if b < 2:
            kept[pl.ds(rows, RANK), at] = m
            to_x[pl.ds(rows, RANK), at] = m
            up_own[b] = up[b]
        else:
            m_y[:RANK, at] = m
            m_xy[:, at] = m
            for i in range(2):
                m_y[pl.ds((b % 2 * 2 + i + 1) * RANK, RANK), :] = up[
                    b, :, pl.ds(i * HALF, HALF)
                ].astype(F32)


def own_sums(scalars, mine, theirs, narrow, wide):
    rows, features = mine.shape
    shapes = [(rows + RANK, HALF), (rows + RANK, HALF), (5 * RANK, HALF), (RANK, HALF)]
    return pl.pallas_call(
        own_kernel,
        out_shape=[jax.ShapeDtypeStruct(s, F32) for s in shapes]
        + [jax.ShapeDtypeStruct((2, RANK, 2 * HALF), BF16)],
        in_specs=[IN_SMEM] * 2 + [IN_ANY] * (4 + len(wide)),
        out_specs=[IN_VMEM] * 5,
        scratch_shapes=[
            pltpu.VMEM((2 * HALF, features), BF16),
            pltpu.VMEM((4, RANK, features), BF16),
            pltpu.VMEM((4, RANK, 2 * HALF), BF16),
            pltpu.VMEM((2 * rows, features), BF16),
            pltpu.SemaphoreType.DMA((2 * DEPTH,)),
            pltpu.SemaphoreType.DMA((8,)),
            pltpu.SemaphoreType.DMA((2,)),
        ],
        compiler_params=pltpu.CompilerParams(vmem_limit_bytes=VMEM),
        cost_estimate=pl.CostEstimate(flops=0, bytes_accessed=0, transcendentals=0),
    )(*scalars, mine, theirs, *narrow, *wide)


def final_kernel(kept, up_own, from_x, from_y, from_xy, m_y, m_xy, out):
    _, z_low, y, _, _ = place()
    line = pl.ds(out.shape[0], RANK)
    m = (kept[line, :] + from_x[line, :]) + (m_y[:RANK, :] + m_xy[...])
    mid = m.T.astype(BF16)
    up = []
    for b in range(2):
        for i in range(UP_TILES):
            lines = pl.ds((b * 2 + i // 2 + 1) * RANK, RANK)
            got = m_y[lines, pl.ds(i % 2 * LANES, LANES)].astype(BF16)
            up.append(up_own[b, :, pl.ds(i * LANES, LANES)] + got)
    for tile in range(2):
        cols = pl.ds(tile * LANES, LANES)
        for side in range(2):
            j = 2 * (z_low ^ tile) + (y ^ side)
            lanes = pl.ds(pl.multiple_of(j * LANES, LANES), LANES)
            for b in range(2):
                span = pl.ds(b * BLK, BLK)
                if side == 0:
                    base = kept[span, cols] + from_x[span, cols]
                else:
                    base = from_y[span, cols] + from_xy[span, cols]
                picked = jnp.zeros((RANK, LANES), BF16)
                for i in range(UP_TILES):
                    picked = jnp.where(j == i, up[b * UP_TILES + i], picked)
                extra = jnp.dot(
                    mid[b * BLK : (b + 1) * BLK], picked, preferred_element_type=F32
                )
                out[span, lanes] = (base + extra).astype(BF16)


def final(*args):
    rows = args[0].shape[0] - RANK
    return pl.pallas_call(
        final_kernel,
        out_shape=jax.ShapeDtypeStruct((rows, 2 * HALF), BF16),
        in_specs=[IN_VMEM] * len(args),
        out_specs=IN_VMEM,
        compiler_params=pltpu.CompilerParams(vmem_limit_bytes=VMEM),
    )(*args)


def make_body(tensor, adapters):
    over_tensor, over_adapter = swaps(tensor, adapters)
    tie = lax.optimization_barrier

    def over_both(array):
        pairs = [
            (i * adapters + j, (i ^ 2) * adapters + (j ^ 1))
            for i in range(tensor)
            for j in range(adapters)
        ]
        return lax.ppermute(array, ("tensor", "adapter"), perm=pairs)

    def body(hidden, value, down, up, chosen, live):
        features = hidden.shape[1]
        w0, down = value.T, down.transpose(0, 2, 1).reshape(RANK, features)
        theirs = over_tensor(hidden, 2)
        w2, w1 = over_tensor(w0, 8), over_tensor(w0, 4)
        v0 = over_tensor(w0, 1)
        v0, down = tie((v0, down))
        d0, ids = prep(chosen, live, down, up[0])
        v1, w0 = over_tensor(w1, 1), over_tensor(v0, 1)
        w2, v1, w0, d0, ids = tie((w2, v1, w0, d0, ids))
        w3, v2 = over_tensor(w2, 4), over_tensor(w2, 1)
        d2, d1 = over_tensor(d0, 8), over_tensor(d0, 4)
        w3, v2, d2, d1, ids, theirs = tie((w3, v2, d2, d1, ids, theirs))
        v3 = over_tensor(w3, 1)
        d3 = over_tensor(d2, 4)
        ids_p = over_tensor(ids, 2)
        wide = (w0, v0, w1, v1, w2, v2, w3, v3)
        theirs, ids_p = tie((theirs, ids_p))
        to_y, to_xy = their_sums(theirs, wide)
        to_y, to_xy, d3 = tie((to_y, to_xy, d3))
        from_y, from_xy = over_tensor(to_y, 2), over_both(to_xy)
        narrow = jnp.concatenate([d0, d1, d2, d3])
        narrow_v = over_tensor(narrow, 1)
        kept, to_x, m_y, m_xy, up_own = own_sums(
            (ids, ids_p), hidden, theirs, (narrow, narrow_v), wide
        )
        from_x, m_y, m_xy = over_adapter(to_x, 1), over_tensor(m_y, 2), over_both(m_xy)
        return final(kept, up_own, from_x, from_y, from_xy, m_y, m_xy)

    return body


def solution(mesh):
    in_specs = (
        P(("groups", "tensor"), "adapter"),
        P("adapter", "tensor"),
        P("tensor", "adapter", None),
        P("tensor", None, None),
        P(("groups", "tensor")),
        P(("groups", "tensor")),
    )
    out_specs = P(("groups", "tensor"), "adapter")
    tensor, adapters = mesh.shape["tensor"], mesh.shape["adapter"]

    def run(hidden, value, down, up, chosen, live):
        blocks = chosen.shape[0] // (mesh.shape["groups"] * tensor)
        fits = (tensor, adapters, blocks) == (4 * DEPTH, 2, 2)
        fits = fits and up.shape == (tensor, RANK, tensor * WIDTH)
        make = make_body if fits else make_general_body
        body = make(tensor, adapters)
        mapped = jax.shard_map(
            body, mesh=mesh, in_specs=in_specs, out_specs=out_specs, check_vma=False
        )
        return mapped(hidden, value, down, up, chosen, live)

    return run
```

```python
import jax
import jax.numpy as jnp
from jax import lax
from jax.experimental import pallas as pl
from jax.experimental.pallas import tpu as pltpu
from jax.sharding import PartitionSpec as P

BLK = 128
LANES = 128
F32 = jnp.float32
BF16 = jnp.bfloat16
MIB = 1 << 20


def dot_nt(a, b):
    return lax.dot_general(a, b, (((1,), (1,)), ((), ())), preferred_element_type=F32)


def swaps(tensor, adapters):
    def over_tensor(array, flip):
        return lax.ppermute(array, "tensor", perm=[(i, i ^ flip) for i in range(tensor)])

    def over_adapter(array, flip):
        return lax.ppermute(array, "adapter", perm=[(i, i ^ flip) for i in range(adapters)])

    return over_tensor, over_adapter


def make_general_body(tensor, adapters):
    depth = tensor // 4
    low = depth // adapters
    over_tensor, over_adapter = swaps(tensor, adapters)

    def body(hidden, value, down, up, chosen, live):
        t, x = lax.axis_index("tensor"), lax.axis_index("adapter")
        z, y, core = t // 4, (t // 2) % 2, t % 2
        rows, features = hidden.shape
        width = value.shape[1]
        homes, rank, wide = up.shape
        blocks = rows // BLK

        theirs = over_tensor(hidden, 2)
        packet = jnp.concatenate([value.T, down.transpose(0, 2, 1).reshape(homes * rank, features)])
        units = {0: packet}
        bit = depth // 2
        while bit:
            units.update({a ^ bit: over_tensor(u, 4 * bit) for a, u in units.items()})
            bit //= 2
        pairs = {a: (u, over_tensor(u, 1)) for a, u in units.items()}

        ids = jnp.stack([chosen, live])
        ids = jnp.concatenate([ids, over_tensor(ids, 2)], axis=1)
        ups = lax.dynamic_slice_in_dim(up, x * (wide // adapters), wide // adapters, 2)[None]
        bit = 1
        while bit < tensor:
            ups = jnp.concatenate([ups, over_tensor(ups, bit)])
            bit *= 2

        w_all = jnp.concatenate([u[:width] for a in range(depth) for u in pairs[a]])
        d_all = jnp.concatenate([u[width:] for a in range(depth) for u in pairs[a]])

        relative = (ids[0] // homes) ^ t
        here = (relative & 2) == 0
        slot = (relative // 4) * 2 + relative % 2
        which = slot * homes + ids[0] % homes

        ups = ups.reshape(tensor, homes, rank, low, 2, 2, width)
        ups = lax.dynamic_index_in_dim(ups, y, 4, keepdims=False)
        z_low = z % low
        order = [lax.dynamic_index_in_dim(ups, z_low ^ a, 3, keepdims=False) for a in range(low)]
        ups = jnp.stack(order, axis=3)
        ups = jnp.where(core == 1, ups[..., ::-1, :], ups)
        ups = ups.reshape(tensor * homes, rank, low * 2 * width)
        up_index = relative * homes + ids[0] % homes

        part = (z // low) ^ x

        def work(x_rows, b0):
            count = x_rows.shape[0] // BLK
            base = dot_nt(x_rows, w_all).reshape(-1, adapters, low * 2 * width)
            kept = lax.dynamic_index_in_dim(base, part, 1, keepdims=False)
            for k in range(1, adapters):
                sent = lax.dynamic_index_in_dim(base, part ^ k, 1, keepdims=False)
                kept = kept + over_adapter(sent, k)
            shrink = dot_nt(x_rows, d_all).reshape(count, BLK, -1, rank)
            spots = jnp.arange(shrink.shape[2], dtype=jnp.int32)
            hot = (which[b0 : b0 + count, None] == spots) & here[b0 : b0 + count, None]
            alive = jnp.arange(BLK, dtype=jnp.int32) < ids[1, b0 : b0 + count, None]
            mask = hot[:, None, :, None] & alive[:, :, None, None]
            return kept, jnp.where(mask, shrink, 0.0).sum(axis=2)

        def finish(kept, shrink, b0):
            mid = shrink.astype(BF16)
            picked = [
                lax.dynamic_index_in_dim(ups, up_index[b], 0, keepdims=False)
                for b in range(b0, b0 + shrink.shape[0])
            ]
            extra = jnp.einsum("bir,brv->biv", mid, jnp.stack(picked), preferred_element_type=F32)
            return (kept + extra.reshape(kept.shape)).astype(BF16)

        kept_own, m_own = work(hidden, 0)
        kept_their, m_their = work(theirs, blocks)
        m = jnp.concatenate([m_own, m_their])
        total = m
        for k in range(1, adapters):
            total = total + over_adapter(m, k)
        m = total.astype(BF16)
        swapped = over_tensor(m, 2)
        m = m + jnp.concatenate([swapped[blocks:], swapped[:blocks]])
        out_their = over_tensor(finish(kept_their, m[blocks:], blocks), 2)
        out_own = finish(kept_own, m[:blocks], 0)
        pair = jnp.stack([out_own, out_their], axis=1)
        pair = pair.reshape(rows, 2, low, 2, width)
        pair = jnp.where(y == 1, pair[:, ::-1], pair)
        pair = jnp.where(core == 1, pair[:, :, :, ::-1], pair)
        pair = jnp.stack(
            [lax.dynamic_index_in_dim(pair, z_low ^ a, 2, keepdims=False) for a in range(low)],
            axis=1,
        )
        return pair.reshape(rows, wide // adapters)

    return body


RANK = 16
WIDTH = 64
DEPTH = 4
TILE = 2 * WIDTH
HALF = 2 * TILE
UP_TILES = 4
VMEM = 16 * MIB
IN_SMEM = pl.BlockSpec(memory_space=pltpu.SMEM)
IN_VMEM = pl.BlockSpec(memory_space=pltpu.VMEM)
IN_HBM = pl.BlockSpec(memory_space=pltpu.HBM)
IN_ANY = pl.BlockSpec(memory_space=pl.ANY)


def place():
    t = lax.axis_index("tensor")
    z, y, core = t // 4, (t // 2) % 2, t % 2
    part = (z // 2) ^ lax.axis_index("adapter")
    return t, z % 2, y, core, part


def gather_wide(wide, w, sems):
    _, _, _, core, part = place()
    copies = []
    for a in range(DEPTH):
        base = ((a // 2) ^ part) * HALF + (a % 2) * TILE
        last = a == DEPTH - 1
        for k in range(2):
            start = pl.multiple_of(base + (core ^ k) * WIDTH, WIDTH)
            copies.append(
                pltpu.make_async_copy(
                    wide[2 * k + last].at[pl.ds(0 if last else a * WIDTH, WIDTH)],
                    w.at[pl.ds(start, WIDTH), :],
                    sems.at[2 * a + k],
                )
            )
    for c in copies:
        c.start()
    return copies


def load_rows(pieces, rows_in, sems):
    at, copies = 0, []
    for i, ref in enumerate(pieces):
        copies.append(
            pltpu.make_async_copy(ref, rows_in.at[pl.ds(at, ref.shape[0])], sems.at[i])
        )
        at += ref.shape[0]
    for c in copies:
        c.start()
    return copies


def base_kernel(rows_ref, *refs):
    wide, (kept, sent, w, rows_in, w_sem, r_sem) = refs[:4], refs[4:]
    copies = load_rows((rows_ref,), rows_in, r_sem) + gather_wide(wide, w, w_sem)
    for c in copies:
        c.wait()
    sent[...] = dot_nt(rows_in[...], w[pl.ds(HALF, HALF), :])
    kept[...] = dot_nt(rows_in[...], w[pl.ds(0, HALF), :])


def base_sums(rows_in, wide):
    rows, features = rows_in.shape
    return pl.pallas_call(
        base_kernel,
        out_shape=[jax.ShapeDtypeStruct((rows, HALF), F32)] * 2,
        in_specs=[IN_ANY] * (1 + len(wide)),
        out_specs=[IN_VMEM] * 2,
        scratch_shapes=[
            pltpu.VMEM((2 * HALF, features), BF16),
            pltpu.VMEM((rows, features), BF16),
            pltpu.SemaphoreType.DMA((2 * DEPTH,)),
            pltpu.SemaphoreType.DMA((1,)),
        ],
        compiler_params=pltpu.CompilerParams(vmem_limit_bytes=9 * MIB),
        cost_estimate=pl.CostEstimate(flops=0, bytes_accessed=0, transcendentals=0),
    )(rows_in, *wide)


def own_kernel(ids, ids_p, mine, theirs, *refs):
    wide, narrow, refs = refs[:4], refs[4:8], refs[8:]
    kept, to_x, m_y, m_xy, up_own, w, d, up, rows_in, w_sem, d_sem, r_sem = refs
    t = lax.axis_index("tensor")
    rows, features = mine.shape
    cols = pl.ds(0, features)
    copies = load_rows((mine, theirs), rows_in, r_sem) + gather_wide(wide, w, w_sem)

    def fetch(b, ref, line):
        lines = pl.ds(line, RANK)
        return [
            pltpu.make_async_copy(ref.at[lines, cols], d.at[b], d_sem.at[2 * b]),
            pltpu.make_async_copy(
                ref.at[lines, pl.ds(features, 2 * HALF)], up.at[b], d_sem.at[2 * b + 1]
            ),
        ]

    where = []
    for b in range(4):
        relative = (ids[b] if b < 2 else ids_p[b - 2]) ^ t
        here = ((relative // 2) % 2) == 0
        unit, other = relative // 4, relative % 2
        where.append(here)

        @pl.when(jnp.logical_not(here))
        def _():
            d[b] = jnp.zeros_like(d[b])
            up[b] = jnp.zeros_like(up[b])

        for i, ref in enumerate(narrow):
            last = i >= 2

            @pl.when(here & (other == i % 2) & ((unit == DEPTH - 1) == last))
            def _():
                line = 0 if last else pl.multiple_of(unit * RANK, RANK)
                for c in fetch(b, ref, line):
                    c.start()

    for c in copies:
        c.wait()
    to_x[:rows, :] = dot_nt(rows_in[pl.ds(0, rows), :], w[pl.ds(HALF, HALF), :])
    kept[:rows, :] = dot_nt(rows_in[pl.ds(0, rows), :], w[pl.ds(0, HALF), :])
    for b, here in enumerate(where):

        @pl.when(here)
        def _():
            for c in fetch(b, narrow[2], 0):
                c.wait()

    for b in range(4):
        at = pl.ds(b % 2 * BLK, BLK)
        m = dot_nt(d[b], rows_in[pl.ds(b * BLK, BLK), :])
        limit = ids[2 + b] if b < 2 else ids_p[b]
        m = jnp.where(lax.broadcasted_iota(jnp.int32, m.shape, 1) < limit, m, 0.0)
        if b < 2:
            kept[pl.ds(rows, RANK), at] = m
            to_x[pl.ds(rows, RANK), at] = m
            up_own[b] = up[b]
        else:
            m_y[:RANK, at] = m
            m_xy[:, at] = m
            for i in range(2):
                m_y[pl.ds((b % 2 * 2 + i + 1) * RANK, RANK), :] = up[
                    b, :, pl.ds(i * HALF, HALF)
                ].astype(F32)


def own_sums(scalars, mine, theirs, narrow, wide):
    rows, features = mine.shape
    shapes = [(rows + RANK, HALF), (rows + RANK, HALF), (5 * RANK, HALF), (RANK, HALF)]
    return pl.pallas_call(
        own_kernel,
        out_shape=[jax.ShapeDtypeStruct(s, F32) for s in shapes]
        + [jax.ShapeDtypeStruct((2, RANK, 2 * HALF), BF16)],
        in_specs=[IN_SMEM] * 2 + [IN_ANY] * (2 + len(wide) + len(narrow)),
        out_specs=[IN_VMEM] * 5,
        scratch_shapes=[
            pltpu.VMEM((2 * HALF, features), BF16),
            pltpu.VMEM((4, RANK, features), BF16),
            pltpu.VMEM((4, RANK, 2 * HALF), BF16),
            pltpu.VMEM((2 * rows, features), BF16),
            pltpu.SemaphoreType.DMA((2 * DEPTH,)),
            pltpu.SemaphoreType.DMA((8,)),
            pltpu.SemaphoreType.DMA((2,)),
        ],
        compiler_params=pltpu.CompilerParams(vmem_limit_bytes=13 * MIB),
        cost_estimate=pl.CostEstimate(flops=0, bytes_accessed=0, transcendentals=0),
    )(*scalars, mine, theirs, *wide, *narrow)


def add_kernel(a, b, out):
    out[...] = a[...] + b[...]


def add(a, b):
    return pl.pallas_call(
        add_kernel,
        out_shape=jax.ShapeDtypeStruct(a.shape, F32),
        in_specs=[IN_VMEM] * 2,
        out_specs=IN_VMEM,
        compiler_params=pltpu.CompilerParams(vmem_limit_bytes=4 * MIB),
        cost_estimate=pl.CostEstimate(flops=1 << 34, bytes_accessed=32 * MIB, transcendentals=0),
    )(a, b)


def final_kernel(kept, up_own, from_x, other, m_y, m_xy, out):
    _, z_low, y, _, _ = place()
    line = pl.ds(out.shape[0], RANK)
    m = (kept[line, :] + from_x[line, :]) + (m_y[:RANK, :] + m_xy[...])
    mid = m.T.astype(BF16)
    up = []
    for b in range(2):
        for i in range(UP_TILES):
            lines = pl.ds((b * 2 + i // 2 + 1) * RANK, RANK)
            got = m_y[lines, pl.ds(i % 2 * LANES, LANES)].astype(BF16)
            up.append(up_own[b, :, pl.ds(i * LANES, LANES)] + got)
    for tile in range(2):
        cols = pl.ds(tile * LANES, LANES)
        for side in range(2):
            j = 2 * (z_low ^ tile) + (y ^ side)
            lanes = pl.ds(pl.multiple_of(j * LANES, LANES), LANES)
            for b in range(2):
                span = pl.ds(b * BLK, BLK)
                if side == 0:
                    base = kept[span, cols] + from_x[span, cols]
                else:
                    base = other[span, cols]
                picked = jnp.zeros((RANK, LANES), BF16)
                for i in range(UP_TILES):
                    picked = jnp.where(j == i, up[b * UP_TILES + i], picked)
                extra = jnp.dot(
                    mid[b * BLK : (b + 1) * BLK], picked, preferred_element_type=F32
                )
                out[span, lanes] = (base + extra).astype(BF16)


def final(*args):
    rows = args[0].shape[0] - RANK
    return pl.pallas_call(
        final_kernel,
        out_shape=jax.ShapeDtypeStruct((rows, 2 * HALF), BF16),
        in_specs=[IN_VMEM] * len(args),
        out_specs=IN_VMEM,
        compiler_params=pltpu.CompilerParams(vmem_limit_bytes=6 * MIB),
    )(*args)


def make_body(tensor, adapters):
    over_tensor, over_adapter = swaps(tensor, adapters)
    tie = lax.optimization_barrier

    def over_both(array):
        pairs = [
            (i * adapters + j, (i ^ 2) * adapters + (j ^ 1))
            for i in range(tensor)
            for j in range(adapters)
        ]
        return lax.ppermute(array, ("tensor", "adapter"), perm=pairs)

    def body(hidden, value, down, up, chosen, live):
        features = hidden.shape[1]
        w0, down = value.T, down.transpose(0, 2, 1).reshape(RANK, features)
        theirs = over_tensor(hidden, 2)
        w2, w1 = over_tensor(w0, 8), over_tensor(w0, 4)
        half = lax.dynamic_slice_in_dim(up[0], lax.axis_index("adapter") * 2 * HALF, 2 * HALF, 1)
        d0 = jnp.concatenate([down, half], axis=1)
        ids = jnp.concatenate([chosen, live])
        w2, w1, w0 = tie((w2, w1, w0))
        w3 = over_tensor(w2, 4)
        w = jnp.concatenate([w0, w1, w2])
        v = over_tensor(w, 1)
        w3, d0, ids = tie((w3, d0, ids))
        v3 = over_tensor(w3, 1)
        d2, d1 = over_tensor(d0, 8), over_tensor(d0, 4)
        ids_p = over_tensor(ids, 2)
        d2, v3 = tie((d2, v3))
        d3 = over_tensor(d2, 4)
        early = jnp.concatenate([d0, d1, d2])
        wide = (w, w3, v, v3)
        to_y, to_xy = base_sums(theirs, wide)
        to_y, to_xy, ids_p = tie((to_y, to_xy, ids_p))
        other = add(over_tensor(to_y, 2), over_both(to_xy))
        _, d3 = tie((to_y, d3))
        narrow = (early, over_tensor(early, 1), d3, over_tensor(d3, 1))
        kept, to_x, m_y, m_xy, up_own = own_sums(
            (ids, ids_p), hidden, theirs, narrow, wide
        )
        from_x, m_y, m_xy = over_adapter(to_x, 1), over_tensor(m_y, 2), over_both(m_xy)
        return final(kept, up_own, from_x, other, m_y, m_xy)

    return body


def solution(mesh):
    in_specs = (
        P(("groups", "tensor"), "adapter"),
        P("adapter", "tensor"),
        P("tensor", "adapter", None),
        P("tensor", None, None),
        P(("groups", "tensor")),
        P(("groups", "tensor")),
    )
    out_specs = P(("groups", "tensor"), "adapter")
    tensor, adapters = mesh.shape["tensor"], mesh.shape["adapter"]

    def run(hidden, value, down, up, chosen, live):
        blocks = chosen.shape[0] // (mesh.shape["groups"] * tensor)
        fits = (tensor, adapters, blocks) == (4 * DEPTH, 2, 2)
        fits = fits and up.shape == (tensor, RANK, tensor * WIDTH)
        make = make_body if fits else make_general_body
        body = make(tensor, adapters)
        mapped = jax.shard_map(
            body, mesh=mesh, in_specs=in_specs, out_specs=out_specs, check_vma=False
        )
        return mapped(hidden, value, down, up, chosen, live)

    return run
```

```python
import jax
import jax.numpy as jnp
from jax import lax
from jax.experimental import pallas as pl
from jax.experimental.pallas import tpu as pltpu
from jax.sharding import PartitionSpec as P

BLK = 128
LANES = 128
F32 = jnp.float32
BF16 = jnp.bfloat16
MIB = 1 << 20


def dot_nt(a, b):
    return lax.dot_general(a, b, (((1,), (1,)), ((), ())), preferred_element_type=F32)


def swaps(tensor, adapters):
    def over_tensor(array, flip):
        return lax.ppermute(array, "tensor", perm=[(i, i ^ flip) for i in range(tensor)])

    def over_adapter(array, flip):
        return lax.ppermute(array, "adapter", perm=[(i, i ^ flip) for i in range(adapters)])

    return over_tensor, over_adapter


def make_general_body(tensor, adapters):
    depth = tensor // 4
    low = depth // adapters
    over_tensor, over_adapter = swaps(tensor, adapters)

    def body(hidden, value, down, up, chosen, live):
        t, x = lax.axis_index("tensor"), lax.axis_index("adapter")
        z, y, core = t // 4, (t // 2) % 2, t % 2
        rows, features = hidden.shape
        width = value.shape[1]
        homes, rank, wide = up.shape
        blocks = rows // BLK

        theirs = over_tensor(hidden, 2)
        packet = jnp.concatenate([value.T, down.transpose(0, 2, 1).reshape(homes * rank, features)])
        units = {0: packet}
        bit = depth // 2
        while bit:
            units.update({a ^ bit: over_tensor(u, 4 * bit) for a, u in units.items()})
            bit //= 2
        pairs = {a: (u, over_tensor(u, 1)) for a, u in units.items()}

        ids = jnp.stack([chosen, live])
        ids = jnp.concatenate([ids, over_tensor(ids, 2)], axis=1)
        ups = lax.dynamic_slice_in_dim(up, x * (wide // adapters), wide // adapters, 2)[None]
        bit = 1
        while bit < tensor:
            ups = jnp.concatenate([ups, over_tensor(ups, bit)])
            bit *= 2

        w_all = jnp.concatenate([u[:width] for a in range(depth) for u in pairs[a]])
        d_all = jnp.concatenate([u[width:] for a in range(depth) for u in pairs[a]])

        relative = (ids[0] // homes) ^ t
        here = (relative & 2) == 0
        slot = (relative // 4) * 2 + relative % 2
        which = slot * homes + ids[0] % homes

        ups = ups.reshape(tensor, homes, rank, low, 2, 2, width)
        ups = lax.dynamic_index_in_dim(ups, y, 4, keepdims=False)
        z_low = z % low
        order = [lax.dynamic_index_in_dim(ups, z_low ^ a, 3, keepdims=False) for a in range(low)]
        ups = jnp.stack(order, axis=3)
        ups = jnp.where(core == 1, ups[..., ::-1, :], ups)
        ups = ups.reshape(tensor * homes, rank, low * 2 * width)
        up_index = relative * homes + ids[0] % homes

        part = (z // low) ^ x

        def work(x_rows, b0):
            count = x_rows.shape[0] // BLK
            base = dot_nt(x_rows, w_all).reshape(-1, adapters, low * 2 * width)
            kept = lax.dynamic_index_in_dim(base, part, 1, keepdims=False)
            for k in range(1, adapters):
                sent = lax.dynamic_index_in_dim(base, part ^ k, 1, keepdims=False)
                kept = kept + over_adapter(sent, k)
            shrink = dot_nt(x_rows, d_all).reshape(count, BLK, -1, rank)
            spots = jnp.arange(shrink.shape[2], dtype=jnp.int32)
            hot = (which[b0 : b0 + count, None] == spots) & here[b0 : b0 + count, None]
            alive = jnp.arange(BLK, dtype=jnp.int32) < ids[1, b0 : b0 + count, None]
            mask = hot[:, None, :, None] & alive[:, :, None, None]
            return kept, jnp.where(mask, shrink, 0.0).sum(axis=2)

        def finish(kept, shrink, b0):
            mid = shrink.astype(BF16)
            picked = [
                lax.dynamic_index_in_dim(ups, up_index[b], 0, keepdims=False)
                for b in range(b0, b0 + shrink.shape[0])
            ]
            extra = jnp.einsum("bir,brv->biv", mid, jnp.stack(picked), preferred_element_type=F32)
            return (kept + extra.reshape(kept.shape)).astype(BF16)

        kept_own, m_own = work(hidden, 0)
        kept_their, m_their = work(theirs, blocks)
        m = jnp.concatenate([m_own, m_their])
        total = m
        for k in range(1, adapters):
            total = total + over_adapter(m, k)
        m = total.astype(BF16)
        swapped = over_tensor(m, 2)
        m = m + jnp.concatenate([swapped[blocks:], swapped[:blocks]])
        out_their = over_tensor(finish(kept_their, m[blocks:], blocks), 2)
        out_own = finish(kept_own, m[:blocks], 0)
        pair = jnp.stack([out_own, out_their], axis=1)
        pair = pair.reshape(rows, 2, low, 2, width)
        pair = jnp.where(y == 1, pair[:, ::-1], pair)
        pair = jnp.where(core == 1, pair[:, :, :, ::-1], pair)
        pair = jnp.stack(
            [lax.dynamic_index_in_dim(pair, z_low ^ a, 2, keepdims=False) for a in range(low)],
            axis=1,
        )
        return pair.reshape(rows, wide // adapters)

    return body


RANK = 16
WIDTH = 64
DEPTH = 4
TILE = 2 * WIDTH
HALF = 2 * TILE
UP_TILES = 4
VMEM = 16 * MIB
IN_SMEM = pl.BlockSpec(memory_space=pltpu.SMEM)
IN_VMEM = pl.BlockSpec(memory_space=pltpu.VMEM)
IN_HBM = pl.BlockSpec(memory_space=pltpu.HBM)
IN_ANY = pl.BlockSpec(memory_space=pl.ANY)


def place():
    t = lax.axis_index("tensor")
    z, y, core = t // 4, (t // 2) % 2, t % 2
    part = (z // 2) ^ lax.axis_index("adapter")
    return t, z % 2, y, core, part


def gather_wide(wide, w, sems):
    _, _, _, core, part = place()
    copies = []
    for a in range(DEPTH):
        base = ((a // 2) ^ part) * HALF + (a % 2) * TILE
        last = a == DEPTH - 1
        for k in range(2):
            start = pl.multiple_of(base + (core ^ k) * WIDTH, WIDTH)
            copies.append(
                pltpu.make_async_copy(
                    wide[2 * k + last].at[pl.ds(0 if last else a * WIDTH, WIDTH)],
                    w.at[pl.ds(start, WIDTH), :],
                    sems.at[2 * a + k],
                )
            )
    for c in copies:
        c.start()
    return copies


def load_rows(pieces, rows_in, sems):
    at, copies = 0, []
    for i, ref in enumerate(pieces):
        copies.append(
            pltpu.make_async_copy(ref, rows_in.at[pl.ds(at, ref.shape[0])], sems.at[i])
        )
        at += ref.shape[0]
    for c in copies:
        c.start()
    return copies


def base_kernel(rows_ref, *refs):
    wide, (kept, sent, w, rows_in, w_sem, r_sem) = refs[:4], refs[4:]
    copies = load_rows((rows_ref,), rows_in, r_sem) + gather_wide(wide, w, w_sem)
    for c in copies:
        c.wait()
    sent[...] = dot_nt(rows_in[...], w[pl.ds(HALF, HALF), :])
    kept[...] = dot_nt(rows_in[...], w[pl.ds(0, HALF), :])


def base_sums(rows_in, wide):
    rows, features = rows_in.shape
    return pl.pallas_call(
        base_kernel,
        out_shape=[jax.ShapeDtypeStruct((rows, HALF), F32)] * 2,
        in_specs=[IN_ANY] * (1 + len(wide)),
        out_specs=[IN_VMEM] * 2,
        scratch_shapes=[
            pltpu.VMEM((2 * HALF, features), BF16),
            pltpu.VMEM((rows, features), BF16),
            pltpu.SemaphoreType.DMA((2 * DEPTH,)),
            pltpu.SemaphoreType.DMA((1,)),
        ],
        compiler_params=pltpu.CompilerParams(vmem_limit_bytes=9 * MIB),
        cost_estimate=pl.CostEstimate(flops=0, bytes_accessed=0, transcendentals=0),
    )(rows_in, *wide)


def own_kernel(ids, ids_p, mine, theirs, *refs):
    wide, narrow, refs = refs[:4], refs[4:6], refs[6:]
    kept, to_x, m_y, m_xy, up_own, w, d, up, rows_in, w_sem, d_sem, r_sem = refs
    t = lax.axis_index("tensor")
    rows, features = mine.shape
    cols = pl.ds(0, features)
    copies = load_rows((mine, theirs), rows_in, r_sem) + gather_wide(wide, w, w_sem)

    def fetch(b, ref, line):
        lines = pl.ds(line, RANK)
        return [
            pltpu.make_async_copy(ref.at[lines, cols], d.at[b], d_sem.at[2 * b]),
            pltpu.make_async_copy(
                ref.at[lines, pl.ds(features, 2 * HALF)], up.at[b], d_sem.at[2 * b + 1]
            ),
        ]

    where = []
    for b in range(4):
        relative = (ids[b] if b < 2 else ids_p[b - 2]) ^ t
        here = ((relative // 2) % 2) == 0
        unit, other = relative // 4, relative % 2
        where.append(here)

        @pl.when(jnp.logical_not(here))
        def _():
            d[b] = jnp.zeros_like(d[b])
            up[b] = jnp.zeros_like(up[b])

        for i, ref in enumerate(narrow):

            @pl.when(here & (other == i))
            def _():
                for c in fetch(b, ref, pl.multiple_of(unit * RANK, RANK)):
                    c.start()

    for c in copies:
        c.wait()
    to_x[:rows, :] = dot_nt(rows_in[pl.ds(0, rows), :], w[pl.ds(HALF, HALF), :])
    kept[:rows, :] = dot_nt(rows_in[pl.ds(0, rows), :], w[pl.ds(0, HALF), :])
    for b, here in enumerate(where):

        @pl.when(here)
        def _():
            for c in fetch(b, narrow[0], 0):
                c.wait()

    for b in range(4):
        at = pl.ds(b % 2 * BLK, BLK)
        m = dot_nt(d[b], rows_in[pl.ds(b * BLK, BLK), :])
        limit = ids[2 + b] if b < 2 else ids_p[b]
        m = jnp.where(lax.broadcasted_iota(jnp.int32, m.shape, 1) < limit, m, 0.0)
        if b < 2:
            kept[pl.ds(rows, RANK), at] = m
            to_x[pl.ds(rows, RANK), at] = m
            up_own[b] = up[b]
        else:
            m_y[:RANK, at] = m
            m_xy[:, at] = m
            for i in range(2):
                m_y[pl.ds((b % 2 * 2 + i + 1) * RANK, RANK), :] = up[
                    b, :, pl.ds(i * HALF, HALF)
                ].astype(F32)


def own_sums(scalars, mine, theirs, narrow, wide):
    rows, features = mine.shape
    shapes = [(rows + RANK, HALF), (rows + RANK, HALF), (5 * RANK, HALF), (RANK, HALF)]
    return pl.pallas_call(
        own_kernel,
        out_shape=[jax.ShapeDtypeStruct(s, F32) for s in shapes]
        + [jax.ShapeDtypeStruct((2, RANK, 2 * HALF), BF16)],
        in_specs=[IN_SMEM] * 2 + [IN_ANY] * (2 + len(wide) + len(narrow)),
        out_specs=[IN_VMEM] * 5,
        scratch_shapes=[
            pltpu.VMEM((2 * HALF, features), BF16),
            pltpu.VMEM((4, RANK, features), BF16),
            pltpu.VMEM((4, RANK, 2 * HALF), BF16),
            pltpu.VMEM((2 * rows, features), BF16),
            pltpu.SemaphoreType.DMA((2 * DEPTH,)),
            pltpu.SemaphoreType.DMA((8,)),
            pltpu.SemaphoreType.DMA((2,)),
        ],
        compiler_params=pltpu.CompilerParams(vmem_limit_bytes=13 * MIB),
        cost_estimate=pl.CostEstimate(flops=0, bytes_accessed=0, transcendentals=0),
    )(*scalars, mine, theirs, *wide, *narrow)


def add_kernel(a, b, out):
    out[...] = a[...] + b[...]


def add(a, b):
    return pl.pallas_call(
        add_kernel,
        out_shape=jax.ShapeDtypeStruct(a.shape, F32),
        in_specs=[IN_VMEM] * 2,
        out_specs=IN_VMEM,
        compiler_params=pltpu.CompilerParams(vmem_limit_bytes=4 * MIB),
        cost_estimate=pl.CostEstimate(flops=1 << 34, bytes_accessed=32 * MIB, transcendentals=0),
    )(a, b)


def final_kernel(kept, up_own, from_x, other, m_y, m_xy, out):
    _, z_low, y, _, _ = place()
    line = pl.ds(out.shape[0], RANK)
    m = (kept[line, :] + from_x[line, :]) + (m_y[:RANK, :] + m_xy[...])
    mid = m.T.astype(BF16)
    up = []
    for b in range(2):
        for i in range(UP_TILES):
            lines = pl.ds((b * 2 + i // 2 + 1) * RANK, RANK)
            got = m_y[lines, pl.ds(i % 2 * LANES, LANES)].astype(BF16)
            up.append(up_own[b, :, pl.ds(i * LANES, LANES)] + got)
    for tile in range(2):
        cols = pl.ds(tile * LANES, LANES)
        for side in range(2):
            j = 2 * (z_low ^ tile) + (y ^ side)
            lanes = pl.ds(pl.multiple_of(j * LANES, LANES), LANES)
            for b in range(2):
                span = pl.ds(b * BLK, BLK)
                if side == 0:
                    base = kept[span, cols] + from_x[span, cols]
                else:
                    base = other[span, cols]
                picked = jnp.zeros((RANK, LANES), BF16)
                for i in range(UP_TILES):
                    picked = jnp.where(j == i, up[b * UP_TILES + i], picked)
                extra = jnp.dot(
                    mid[b * BLK : (b + 1) * BLK], picked, preferred_element_type=F32
                )
                out[span, lanes] = (base + extra).astype(BF16)


def final(*args):
    rows = args[0].shape[0] - RANK
    return pl.pallas_call(
        final_kernel,
        out_shape=jax.ShapeDtypeStruct((rows, 2 * HALF), BF16),
        in_specs=[IN_VMEM] * len(args),
        out_specs=IN_VMEM,
        compiler_params=pltpu.CompilerParams(vmem_limit_bytes=6 * MIB),
    )(*args)


def make_body(tensor, adapters):
    over_tensor, over_adapter = swaps(tensor, adapters)
    tie = lax.optimization_barrier

    def over_both(array):
        pairs = [
            (i * adapters + j, (i ^ 2) * adapters + (j ^ 1))
            for i in range(tensor)
            for j in range(adapters)
        ]
        return lax.ppermute(array, ("tensor", "adapter"), perm=pairs)

    def body(hidden, value, down, up, chosen, live):
        features = hidden.shape[1]
        w0, down = value.T, down.transpose(0, 2, 1).reshape(RANK, features)
        theirs = over_tensor(hidden, 2)
        w2, w1 = over_tensor(w0, 8), over_tensor(w0, 4)
        half = lax.dynamic_slice_in_dim(up[0], lax.axis_index("adapter") * 2 * HALF, 2 * HALF, 1)
        d0 = jnp.concatenate([down, half], axis=1)
        ids = jnp.concatenate([chosen, live])
        w2, w1, w0, d0 = tie((w2, w1, w0, d0))
        w3 = over_tensor(w2, 4)
        d2, d1 = over_tensor(d0, 8), over_tensor(d0, 4)
        w = jnp.concatenate([w0, w1, w2])
        v = over_tensor(w, 1)
        d3 = over_tensor(d0, 12)
        w3, d2, d1, d3, ids = tie((w3, d2, d1, d3, ids))
        v3, ids_p = over_tensor(w3, 1), over_tensor(ids, 2)
        narrow = jnp.concatenate([d0, d1, d2, d3])
        narrow_v = over_tensor(narrow, 1)
        wide = (w, w3, v, v3)
        to_y, to_xy = base_sums(theirs, wide)
        to_y, to_xy, ids_p = tie((to_y, to_xy, ids_p))
        other = add(over_tensor(to_y, 2), over_both(to_xy))
        narrow = (narrow, narrow_v)
        kept, to_x, m_y, m_xy, up_own = own_sums(
            (ids, ids_p), hidden, theirs, narrow, wide
        )
        from_x, m_y, m_xy = over_adapter(to_x, 1), over_tensor(m_y, 2), over_both(m_xy)
        return final(kept, up_own, from_x, other, m_y, m_xy)

    return body


def solution(mesh):
    in_specs = (
        P(("groups", "tensor"), "adapter"),
        P("adapter", "tensor"),
        P("tensor", "adapter", None),
        P("tensor", None, None),
        P(("groups", "tensor")),
        P(("groups", "tensor")),
    )
    out_specs = P(("groups", "tensor"), "adapter")
    tensor, adapters = mesh.shape["tensor"], mesh.shape["adapter"]

    def run(hidden, value, down, up, chosen, live):
        blocks = chosen.shape[0] // (mesh.shape["groups"] * tensor)
        fits = (tensor, adapters, blocks) == (4 * DEPTH, 2, 2)
        fits = fits and up.shape == (tensor, RANK, tensor * WIDTH)
        make = make_body if fits else make_general_body
        body = make(tensor, adapters)
        mapped = jax.shard_map(
            body, mesh=mesh, in_specs=in_specs, out_specs=out_specs, check_vma=False
        )
        return mapped(hidden, value, down, up, chosen, live)

    return run
```

```python
import jax
import jax.numpy as jnp
from jax import lax
from jax.experimental import pallas as pl
from jax.experimental.pallas import tpu as pltpu
from jax.sharding import PartitionSpec as P

BLK = 128
LANES = 128
F32 = jnp.float32
BF16 = jnp.bfloat16
MIB = 1 << 20


def dot_nt(a, b):
    return lax.dot_general(a, b, (((1,), (1,)), ((), ())), preferred_element_type=F32)


def swaps(tensor, adapters):
    def over_tensor(array, flip):
        return lax.ppermute(array, "tensor", perm=[(i, i ^ flip) for i in range(tensor)])

    def over_adapter(array, flip):
        return lax.ppermute(array, "adapter", perm=[(i, i ^ flip) for i in range(adapters)])

    return over_tensor, over_adapter


def make_general_body(tensor, adapters):
    depth = tensor // 4
    low = depth // adapters
    over_tensor, over_adapter = swaps(tensor, adapters)

    def body(hidden, value, down, up, chosen, live):
        t, x = lax.axis_index("tensor"), lax.axis_index("adapter")
        z, y, core = t // 4, (t // 2) % 2, t % 2
        rows, features = hidden.shape
        width = value.shape[1]
        homes, rank, wide = up.shape
        blocks = rows // BLK

        theirs = over_tensor(hidden, 2)
        packet = jnp.concatenate([value.T, down.transpose(0, 2, 1).reshape(homes * rank, features)])
        units = {0: packet}
        bit = depth // 2
        while bit:
            units.update({a ^ bit: over_tensor(u, 4 * bit) for a, u in units.items()})
            bit //= 2
        pairs = {a: (u, over_tensor(u, 1)) for a, u in units.items()}

        ids = jnp.stack([chosen, live])
        ids = jnp.concatenate([ids, over_tensor(ids, 2)], axis=1)
        ups = lax.dynamic_slice_in_dim(up, x * (wide // adapters), wide // adapters, 2)[None]
        bit = 1
        while bit < tensor:
            ups = jnp.concatenate([ups, over_tensor(ups, bit)])
            bit *= 2

        w_all = jnp.concatenate([u[:width] for a in range(depth) for u in pairs[a]])
        d_all = jnp.concatenate([u[width:] for a in range(depth) for u in pairs[a]])

        relative = (ids[0] // homes) ^ t
        here = (relative & 2) == 0
        slot = (relative // 4) * 2 + relative % 2
        which = slot * homes + ids[0] % homes

        ups = ups.reshape(tensor, homes, rank, low, 2, 2, width)
        ups = lax.dynamic_index_in_dim(ups, y, 4, keepdims=False)
        z_low = z % low
        order = [lax.dynamic_index_in_dim(ups, z_low ^ a, 3, keepdims=False) for a in range(low)]
        ups = jnp.stack(order, axis=3)
        ups = jnp.where(core == 1, ups[..., ::-1, :], ups)
        ups = ups.reshape(tensor * homes, rank, low * 2 * width)
        up_index = relative * homes + ids[0] % homes

        part = (z // low) ^ x

        def work(x_rows, b0):
            count = x_rows.shape[0] // BLK
            base = dot_nt(x_rows, w_all).reshape(-1, adapters, low * 2 * width)
            kept = lax.dynamic_index_in_dim(base, part, 1, keepdims=False)
            for k in range(1, adapters):
                sent = lax.dynamic_index_in_dim(base, part ^ k, 1, keepdims=False)
                kept = kept + over_adapter(sent, k)
            shrink = dot_nt(x_rows, d_all).reshape(count, BLK, -1, rank)
            spots = jnp.arange(shrink.shape[2], dtype=jnp.int32)
            hot = (which[b0 : b0 + count, None] == spots) & here[b0 : b0 + count, None]
            alive = jnp.arange(BLK, dtype=jnp.int32) < ids[1, b0 : b0 + count, None]
            mask = hot[:, None, :, None] & alive[:, :, None, None]
            return kept, jnp.where(mask, shrink, 0.0).sum(axis=2)

        def finish(kept, shrink, b0):
            mid = shrink.astype(BF16)
            picked = [
                lax.dynamic_index_in_dim(ups, up_index[b], 0, keepdims=False)
                for b in range(b0, b0 + shrink.shape[0])
            ]
            extra = jnp.einsum("bir,brv->biv", mid, jnp.stack(picked), preferred_element_type=F32)
            return (kept + extra.reshape(kept.shape)).astype(BF16)

        kept_own, m_own = work(hidden, 0)
        kept_their, m_their = work(theirs, blocks)
        m = jnp.concatenate([m_own, m_their])
        total = m
        for k in range(1, adapters):
            total = total + over_adapter(m, k)
        m = total.astype(BF16)
        swapped = over_tensor(m, 2)
        m = m + jnp.concatenate([swapped[blocks:], swapped[:blocks]])
        out_their = over_tensor(finish(kept_their, m[blocks:], blocks), 2)
        out_own = finish(kept_own, m[:blocks], 0)
        pair = jnp.stack([out_own, out_their], axis=1)
        pair = pair.reshape(rows, 2, low, 2, width)
        pair = jnp.where(y == 1, pair[:, ::-1], pair)
        pair = jnp.where(core == 1, pair[:, :, :, ::-1], pair)
        pair = jnp.stack(
            [lax.dynamic_index_in_dim(pair, z_low ^ a, 2, keepdims=False) for a in range(low)],
            axis=1,
        )
        return pair.reshape(rows, wide // adapters)

    return body


RANK = 16
WIDTH = 64
DEPTH = 4
TILE = 2 * WIDTH
HALF = 2 * TILE
UP_TILES = 4
VMEM = 16 * MIB
IN_SMEM = pl.BlockSpec(memory_space=pltpu.SMEM)
IN_VMEM = pl.BlockSpec(memory_space=pltpu.VMEM)
IN_HBM = pl.BlockSpec(memory_space=pltpu.HBM)
IN_ANY = pl.BlockSpec(memory_space=pl.ANY)


def place():
    t = lax.axis_index("tensor")
    z, y, core = t // 4, (t // 2) % 2, t % 2
    part = (z // 2) ^ lax.axis_index("adapter")
    return t, z % 2, y, core, part


def gather_wide(wide, w, sems):
    _, _, _, core, part = place()
    copies = []
    for a in range(DEPTH):
        base = ((a // 2) ^ part) * HALF + (a % 2) * TILE
        last = a == DEPTH - 1
        for k in range(2):
            start = pl.multiple_of(base + (core ^ k) * WIDTH, WIDTH)
            copies.append(
                pltpu.make_async_copy(
                    wide[2 * k + last].at[pl.ds(0 if last else a * WIDTH, WIDTH)],
                    w.at[pl.ds(start, WIDTH), :],
                    sems.at[2 * a + k],
                )
            )
    for c in copies:
        c.start()
    return copies


def load_rows(pieces, rows_in, sems):
    at, copies = 0, []
    for i, ref in enumerate(pieces):
        copies.append(
            pltpu.make_async_copy(ref, rows_in.at[pl.ds(at, ref.shape[0])], sems.at[i])
        )
        at += ref.shape[0]
    for c in copies:
        c.start()
    return copies


def base_kernel(rows_in, *refs):
    wide, (kept, sent, w, w_sem) = refs[:4], refs[4:]
    copies = gather_wide(wide, w, w_sem)
    for c in copies:
        c.wait()
    sent[...] = dot_nt(rows_in[...], w[pl.ds(HALF, HALF), :])
    kept[...] = dot_nt(rows_in[...], w[pl.ds(0, HALF), :])


def base_sums(rows_in, wide):
    rows, features = rows_in.shape
    return pl.pallas_call(
        base_kernel,
        out_shape=[jax.ShapeDtypeStruct((rows, HALF), F32)] * 2,
        in_specs=[IN_VMEM] + [IN_ANY] * len(wide),
        out_specs=[IN_VMEM] * 2,
        scratch_shapes=[
            pltpu.VMEM((2 * HALF, features), BF16),
            pltpu.SemaphoreType.DMA((2 * DEPTH,)),
        ],
        compiler_params=pltpu.CompilerParams(vmem_limit_bytes=9 * MIB),
        cost_estimate=pl.CostEstimate(flops=0, bytes_accessed=0, transcendentals=0),
    )(rows_in, *wide)


def own_kernel(ids, ids_p, mine, theirs, *refs):
    wide, narrow, refs = refs[:4], refs[4:6], refs[6:]
    kept, to_x, m_y, m_xy, up_own, w, d, up, rows_in, w_sem, d_sem, r_sem = refs
    t = lax.axis_index("tensor")
    rows, features = mine.shape
    cols = pl.ds(0, features)
    copies = load_rows((mine, theirs), rows_in, r_sem) + gather_wide(wide, w, w_sem)

    def fetch(b, ref, line):
        lines = pl.ds(line, RANK)
        return [
            pltpu.make_async_copy(ref.at[lines, cols], d.at[b], d_sem.at[2 * b]),
            pltpu.make_async_copy(
                ref.at[lines, pl.ds(features, 2 * HALF)], up.at[b], d_sem.at[2 * b + 1]
            ),
        ]

    where = []
    for b in range(4):
        relative = (ids[b] if b < 2 else ids_p[b - 2]) ^ t
        here = ((relative // 2) % 2) == 0
        unit, other = relative // 4, relative % 2
        where.append(here)

        @pl.when(jnp.logical_not(here))
        def _():
            d[b] = jnp.zeros_like(d[b])
            up[b] = jnp.zeros_like(up[b])

        for i, ref in enumerate(narrow):

            @pl.when(here & (other == i))
            def _():
                for c in fetch(b, ref, pl.multiple_of(unit * RANK, RANK)):
                    c.start()

    for c in copies:
        c.wait()
    to_x[:rows, :] = dot_nt(rows_in[pl.ds(0, rows), :], w[pl.ds(HALF, HALF), :])
    kept[:rows, :] = dot_nt(rows_in[pl.ds(0, rows), :], w[pl.ds(0, HALF), :])
    for b, here in enumerate(where):

        @pl.when(here)
        def _():
            for c in fetch(b, narrow[0], 0):
                c.wait()

    for b in range(4):
        at = pl.ds(b % 2 * BLK, BLK)
        m = dot_nt(d[b], rows_in[pl.ds(b * BLK, BLK), :])
        limit = ids[2 + b] if b < 2 else ids_p[b]
        m = jnp.where(lax.broadcasted_iota(jnp.int32, m.shape, 1) < limit, m, 0.0)
        if b < 2:
            kept[pl.ds(rows, RANK), at] = m
            to_x[pl.ds(rows, RANK), at] = m
            up_own[b] = up[b]
        else:
            m_xy[:, at] = m
            for i in range(3):
                part = m.astype(BF16)
                m_y[pl.ds(i * RANK, RANK), at] = part
                m = m - part.astype(F32)
            for i in range(2):
                m_y[pl.ds((b % 2 * 2 + i + 3) * RANK, RANK), :] = up[b, :, pl.ds(i * HALF, HALF)]


def own_sums(scalars, mine, theirs, narrow, wide):
    rows, features = mine.shape
    part, m_xy = ((rows + RANK, HALF), F32), ((RANK, HALF), F32)
    shapes = [part, part, ((7 * RANK, HALF), BF16), m_xy, ((2, RANK, 2 * HALF), BF16)]
    return pl.pallas_call(
        own_kernel,
        out_shape=[jax.ShapeDtypeStruct(*s) for s in shapes],
        in_specs=[IN_SMEM] * 2 + [IN_ANY] * (2 + len(wide) + len(narrow)),
        out_specs=[IN_VMEM] * 5,
        scratch_shapes=[
            pltpu.VMEM((2 * HALF, features), BF16),
            pltpu.VMEM((4, RANK, features), BF16),
            pltpu.VMEM((4, RANK, 2 * HALF), BF16),
            pltpu.VMEM((2 * rows, features), BF16),
            pltpu.SemaphoreType.DMA((2 * DEPTH,)),
            pltpu.SemaphoreType.DMA((8,)),
            pltpu.SemaphoreType.DMA((2,)),
        ],
        compiler_params=pltpu.CompilerParams(vmem_limit_bytes=13 * MIB),
        cost_estimate=pl.CostEstimate(flops=0, bytes_accessed=0, transcendentals=0),
    )(*scalars, mine, theirs, *wide, *narrow)


def add_kernel(a, b, out):
    out[...] = a[...] + b[...]


def add(a, b):
    return pl.pallas_call(
        add_kernel,
        out_shape=jax.ShapeDtypeStruct(a.shape, F32),
        in_specs=[IN_VMEM] * 2,
        out_specs=IN_VMEM,
        compiler_params=pltpu.CompilerParams(vmem_limit_bytes=4 * MIB),
        cost_estimate=pl.CostEstimate(flops=1 << 34, bytes_accessed=32 * MIB, transcendentals=0),
    )(a, b)


def final_kernel(kept, up_own, from_x, other, m_y, m_xy, out):
    _, z_low, y, _, _ = place()
    line = pl.ds(out.shape[0], RANK)
    parts = [m_y[pl.ds(i * RANK, RANK), :].astype(F32) for i in range(3)]
    m = (kept[line, :] + from_x[line, :]) + ((parts[0] + parts[1]) + parts[2] + m_xy[...])
    mid = m.T.astype(BF16)
    up = []
    for b in range(2):
        for i in range(UP_TILES):
            lines = pl.ds((b * 2 + i // 2 + 3) * RANK, RANK)
            got = m_y[lines, pl.ds(i % 2 * LANES, LANES)]
            up.append(up_own[b, :, pl.ds(i * LANES, LANES)] + got)
    for tile in range(2):
        cols = pl.ds(tile * LANES, LANES)
        for side in range(2):
            j = 2 * (z_low ^ tile) + (y ^ side)
            lanes = pl.ds(pl.multiple_of(j * LANES, LANES), LANES)
            for b in range(2):
                span = pl.ds(b * BLK, BLK)
                if side == 0:
                    base = kept[span, cols] + from_x[span, cols]
                else:
                    base = other[span, cols]
                picked = jnp.zeros((RANK, LANES), BF16)
                for i in range(UP_TILES):
                    picked = jnp.where(j == i, up[b * UP_TILES + i], picked)
                extra = jnp.dot(
                    mid[b * BLK : (b + 1) * BLK], picked, preferred_element_type=F32
                )
                out[span, lanes] = (base + extra).astype(BF16)


def final(*args):
    rows = args[0].shape[0] - RANK
    return pl.pallas_call(
        final_kernel,
        out_shape=jax.ShapeDtypeStruct((rows, 2 * HALF), BF16),
        in_specs=[IN_VMEM] * len(args),
        out_specs=IN_VMEM,
        compiler_params=pltpu.CompilerParams(vmem_limit_bytes=6 * MIB),
    )(*args)


def make_body(tensor, adapters):
    over_tensor, over_adapter = swaps(tensor, adapters)
    tie = lax.optimization_barrier

    def over_both(array):
        pairs = [
            (i * adapters + j, (i ^ 2) * adapters + (j ^ 1))
            for i in range(tensor)
            for j in range(adapters)
        ]
        return lax.ppermute(array, ("tensor", "adapter"), perm=pairs)

    def body(hidden, value, down, up, chosen, live):
        features = hidden.shape[1]
        w0, down = value.T, down.transpose(0, 2, 1).reshape(RANK, features)
        theirs = over_tensor(hidden, 2)
        w2, w1 = over_tensor(w0, 8), over_tensor(w0, 4)
        half = lax.dynamic_slice_in_dim(up[0], lax.axis_index("adapter") * 2 * HALF, 2 * HALF, 1)
        d0 = jnp.concatenate([down, half], axis=1)
        ids = jnp.concatenate([chosen, live])
        w2, w1, w0, d0 = tie((w2, w1, w0, d0))
        w3 = over_tensor(w2, 4)
        d2, d1 = over_tensor(d0, 8), over_tensor(d0, 4)
        w = jnp.concatenate([w0, w1, w2])
        v = over_tensor(w, 1)
        d3 = over_tensor(d0, 12)
        d1, d2, d3, w3, ids = tie((d1, d2, d3, w3, ids))
        v3, ids_p = over_tensor(w3, 1), over_tensor(ids, 2)
        narrow = jnp.concatenate([d0, d1, d2, d3])
        narrow_v = over_tensor(narrow, 1)
        wide = (w, w3, v, v3)
        to_y, to_xy = base_sums(theirs, wide)
        to_y, to_xy, ids_p = tie((to_y, to_xy, ids_p))
        other = add(over_tensor(to_y, 2), over_both(to_xy))
        narrow = (narrow, narrow_v)
        kept, to_x, m_y, m_xy, up_own = own_sums(
            (ids, ids_p), hidden, theirs, narrow, wide
        )
        from_x, m_y, m_xy = over_adapter(to_x, 1), over_tensor(m_y, 2), over_both(m_xy)
        return final(kept, up_own, from_x, other, m_y, m_xy)

    return body


def solution(mesh):
    in_specs = (
        P(("groups", "tensor"), "adapter"),
        P("adapter", "tensor"),
        P("tensor", "adapter", None),
        P("tensor", None, None),
        P(("groups", "tensor")),
        P(("groups", "tensor")),
    )
    out_specs = P(("groups", "tensor"), "adapter")
    tensor, adapters = mesh.shape["tensor"], mesh.shape["adapter"]

    def run(hidden, value, down, up, chosen, live):
        blocks = chosen.shape[0] // (mesh.shape["groups"] * tensor)
        fits = (tensor, adapters, blocks) == (4 * DEPTH, 2, 2)
        fits = fits and up.shape == (tensor, RANK, tensor * WIDTH)
        make = make_body if fits else make_general_body
        body = make(tensor, adapters)
        mapped = jax.shard_map(
            body, mesh=mesh, in_specs=in_specs, out_specs=out_specs, check_vma=False
        )
        return mapped(hidden, value, down, up, chosen, live)

    return run
```

```python
import jax
import jax.numpy as jnp
from jax import lax
from jax.experimental import pallas as pl
from jax.experimental.pallas import tpu as pltpu
from jax.sharding import PartitionSpec as P

BLK = 128
LANES = 128
F32 = jnp.float32
BF16 = jnp.bfloat16
MIB = 1 << 20


def dot_nt(a, b):
    return lax.dot_general(a, b, (((1,), (1,)), ((), ())), preferred_element_type=F32)


def swaps(tensor, adapters):
    def over_tensor(array, flip):
        return lax.ppermute(array, "tensor", perm=[(i, i ^ flip) for i in range(tensor)])

    def over_adapter(array, flip):
        return lax.ppermute(array, "adapter", perm=[(i, i ^ flip) for i in range(adapters)])

    return over_tensor, over_adapter


def make_general_body(tensor, adapters):
    depth = tensor // 4
    low = depth // adapters
    over_tensor, over_adapter = swaps(tensor, adapters)

    def body(hidden, value, down, up, chosen, live):
        t, x = lax.axis_index("tensor"), lax.axis_index("adapter")
        z, y, core = t // 4, (t // 2) % 2, t % 2
        rows, features = hidden.shape
        width = value.shape[1]
        homes, rank, wide = up.shape
        blocks = rows // BLK

        theirs = over_tensor(hidden, 2)
        packet = jnp.concatenate([value.T, down.transpose(0, 2, 1).reshape(homes * rank, features)])
        units = {0: packet}
        bit = depth // 2
        while bit:
            units.update({a ^ bit: over_tensor(u, 4 * bit) for a, u in units.items()})
            bit //= 2
        pairs = {a: (u, over_tensor(u, 1)) for a, u in units.items()}

        ids = jnp.stack([chosen, live])
        ids = jnp.concatenate([ids, over_tensor(ids, 2)], axis=1)
        ups = lax.dynamic_slice_in_dim(up, x * (wide // adapters), wide // adapters, 2)[None]
        bit = 1
        while bit < tensor:
            ups = jnp.concatenate([ups, over_tensor(ups, bit)])
            bit *= 2

        w_all = jnp.concatenate([u[:width] for a in range(depth) for u in pairs[a]])
        d_all = jnp.concatenate([u[width:] for a in range(depth) for u in pairs[a]])

        relative = (ids[0] // homes) ^ t
        here = (relative & 2) == 0
        slot = (relative // 4) * 2 + relative % 2
        which = slot * homes + ids[0] % homes

        ups = ups.reshape(tensor, homes, rank, low, 2, 2, width)
        ups = lax.dynamic_index_in_dim(ups, y, 4, keepdims=False)
        z_low = z % low
        order = [lax.dynamic_index_in_dim(ups, z_low ^ a, 3, keepdims=False) for a in range(low)]
        ups = jnp.stack(order, axis=3)
        ups = jnp.where(core == 1, ups[..., ::-1, :], ups)
        ups = ups.reshape(tensor * homes, rank, low * 2 * width)
        up_index = relative * homes + ids[0] % homes

        part = (z // low) ^ x

        def work(x_rows, b0):
            count = x_rows.shape[0] // BLK
            base = dot_nt(x_rows, w_all).reshape(-1, adapters, low * 2 * width)
            kept = lax.dynamic_index_in_dim(base, part, 1, keepdims=False)
            for k in range(1, adapters):
                sent = lax.dynamic_index_in_dim(base, part ^ k, 1, keepdims=False)
                kept = kept + over_adapter(sent, k)
            shrink = dot_nt(x_rows, d_all).reshape(count, BLK, -1, rank)
            spots = jnp.arange(shrink.shape[2], dtype=jnp.int32)
            hot = (which[b0 : b0 + count, None] == spots) & here[b0 : b0 + count, None]
            alive = jnp.arange(BLK, dtype=jnp.int32) < ids[1, b0 : b0 + count, None]
            mask = hot[:, None, :, None] & alive[:, :, None, None]
            return kept, jnp.where(mask, shrink, 0.0).sum(axis=2)

        def finish(kept, shrink, b0):
            mid = shrink.astype(BF16)
            picked = [
                lax.dynamic_index_in_dim(ups, up_index[b], 0, keepdims=False)
                for b in range(b0, b0 + shrink.shape[0])
            ]
            extra = jnp.einsum("bir,brv->biv", mid, jnp.stack(picked), preferred_element_type=F32)
            return (kept + extra.reshape(kept.shape)).astype(BF16)

        kept_own, m_own = work(hidden, 0)
        kept_their, m_their = work(theirs, blocks)
        m = jnp.concatenate([m_own, m_their])
        total = m
        for k in range(1, adapters):
            total = total + over_adapter(m, k)
        m = total.astype(BF16)
        swapped = over_tensor(m, 2)
        m = m + jnp.concatenate([swapped[blocks:], swapped[:blocks]])
        out_their = over_tensor(finish(kept_their, m[blocks:], blocks), 2)
        out_own = finish(kept_own, m[:blocks], 0)
        pair = jnp.stack([out_own, out_their], axis=1)
        pair = pair.reshape(rows, 2, low, 2, width)
        pair = jnp.where(y == 1, pair[:, ::-1], pair)
        pair = jnp.where(core == 1, pair[:, :, :, ::-1], pair)
        pair = jnp.stack(
            [lax.dynamic_index_in_dim(pair, z_low ^ a, 2, keepdims=False) for a in range(low)],
            axis=1,
        )
        return pair.reshape(rows, wide // adapters)

    return body


RANK = 16
WIDTH = 64
DEPTH = 4
TILE = 2 * WIDTH
HALF = 2 * TILE
UP_TILES = 4
VMEM = 16 * MIB
IN_SMEM = pl.BlockSpec(memory_space=pltpu.SMEM)
IN_VMEM = pl.BlockSpec(memory_space=pltpu.VMEM)
IN_HBM = pl.BlockSpec(memory_space=pltpu.HBM)
IN_ANY = pl.BlockSpec(memory_space=pl.ANY)


def place():
    t = lax.axis_index("tensor")
    z, y, core = t // 4, (t // 2) % 2, t % 2
    part = (z // 2) ^ lax.axis_index("adapter")
    return t, z % 2, y, core, part


def gather_wide(wide, w, sems):
    _, _, _, core, part = place()
    copies = []
    for a in range(DEPTH):
        base = ((a // 2) ^ part) * HALF + (a % 2) * TILE
        last = a == DEPTH - 1
        for k in range(2):
            start = pl.multiple_of(base + (core ^ k) * WIDTH, WIDTH)
            copies.append(
                pltpu.make_async_copy(
                    wide[2 * k + last].at[pl.ds(0 if last else a * WIDTH, WIDTH)],
                    w.at[pl.ds(start, WIDTH), :],
                    sems.at[2 * a + k],
                )
            )
    for c in copies:
        c.start()
    return copies


def base_kernel(rows_in, *refs):
    wide, (kept, sent, w, w_sem) = refs[:4], refs[4:]
    copies = gather_wide(wide, w, w_sem)
    for c in copies:
        c.wait()
    sent[...] = dot_nt(rows_in[...], w[pl.ds(HALF, HALF), :])
    kept[...] = dot_nt(rows_in[...], w[pl.ds(0, HALF), :])


def base_sums(rows_in, wide):
    rows, features = rows_in.shape
    return pl.pallas_call(
        base_kernel,
        out_shape=[jax.ShapeDtypeStruct((rows, HALF), F32)] * 2,
        in_specs=[IN_VMEM] + [IN_ANY] * len(wide),
        out_specs=[IN_VMEM] * 2,
        scratch_shapes=[
            pltpu.VMEM((2 * HALF, features), BF16),
            pltpu.SemaphoreType.DMA((2 * DEPTH,)),
        ],
        compiler_params=pltpu.CompilerParams(vmem_limit_bytes=9 * MIB),
        cost_estimate=pl.CostEstimate(flops=0, bytes_accessed=0, transcendentals=0),
    )(rows_in, *wide)


def own_kernel(ids, ids_p, mine, theirs, *refs):
    wide, narrow, refs = refs[:4], refs[4:6], refs[6:]
    kept, to_x, m_y, m_xy, up_own, w, d, up, w_sem, d_sem = refs
    t = lax.axis_index("tensor")
    rows, features = mine.shape
    cols = pl.ds(0, features)
    copies = gather_wide(wide, w, w_sem)

    def fetch(b, ref, line):
        lines = pl.ds(line, RANK)
        return [
            pltpu.make_async_copy(ref.at[lines, cols], d.at[b], d_sem.at[2 * b]),
            pltpu.make_async_copy(
                ref.at[lines, pl.ds(features, 2 * HALF)], up.at[b], d_sem.at[2 * b + 1]
            ),
        ]

    where = []
    for b in range(4):
        relative = (ids[b] if b < 2 else ids_p[b - 2]) ^ t
        here = ((relative // 2) % 2) == 0
        unit, other = relative // 4, relative % 2
        where.append(here)

        @pl.when(jnp.logical_not(here))
        def _():
            d[b] = jnp.zeros_like(d[b])
            up[b] = jnp.zeros_like(up[b])

        for i, ref in enumerate(narrow):

            @pl.when(here & (other == i))
            def _():
                for c in fetch(b, ref, pl.multiple_of(unit * RANK, RANK)):
                    c.start()

    for c in copies:
        c.wait()
    to_x[:rows, :] = dot_nt(mine[...], w[pl.ds(HALF, HALF), :])
    kept[:rows, :] = dot_nt(mine[...], w[pl.ds(0, HALF), :])
    for b, here in enumerate(where):

        @pl.when(here)
        def _():
            for c in fetch(b, narrow[0], 0):
                c.wait()

    for b in range(4):
        at = pl.ds(b % 2 * BLK, BLK)
        m = dot_nt(d[b], (mine if b < 2 else theirs)[at, :])
        limit = ids[2 + b] if b < 2 else ids_p[b]
        m = jnp.where(lax.broadcasted_iota(jnp.int32, m.shape, 1) < limit, m, 0.0)
        if b < 2:
            kept[pl.ds(rows, RANK), at] = m
            to_x[pl.ds(rows, RANK), at] = m
            up_own[b] = up[b]
        else:
            m_xy[:, at] = m
            for i in range(3):
                part = m.astype(BF16)
                m_y[pl.ds(i * RANK, RANK), at] = part
                m = m - part.astype(F32)
            for i in range(2):
                m_y[pl.ds((b % 2 * 2 + i + 3) * RANK, RANK), :] = up[b, :, pl.ds(i * HALF, HALF)]


def own_sums(scalars, mine, theirs, narrow, wide):
    rows, features = mine.shape
    part, m_xy = ((rows + RANK, HALF), F32), ((RANK, HALF), F32)
    shapes = [part, part, ((7 * RANK, HALF), BF16), m_xy, ((2, RANK, 2 * HALF), BF16)]
    return pl.pallas_call(
        own_kernel,
        out_shape=[jax.ShapeDtypeStruct(*s) for s in shapes],
        in_specs=[IN_SMEM] * 2 + [IN_VMEM] * 2 + [IN_ANY] * (len(wide) + len(narrow)),
        out_specs=[IN_VMEM] * 5,
        scratch_shapes=[
            pltpu.VMEM((2 * HALF, features), BF16),
            pltpu.VMEM((4, RANK, features), BF16),
            pltpu.VMEM((4, RANK, 2 * HALF), BF16),
            pltpu.SemaphoreType.DMA((2 * DEPTH,)),
            pltpu.SemaphoreType.DMA((8,)),
        ],
        compiler_params=pltpu.CompilerParams(vmem_limit_bytes=9 * MIB),
        cost_estimate=pl.CostEstimate(flops=0, bytes_accessed=0, transcendentals=0),
    )(*scalars, mine, theirs, *wide, *narrow)


def add_kernel(a, b, out):
    out[...] = a[...] + b[...]


def add(a, b):
    return pl.pallas_call(
        add_kernel,
        out_shape=jax.ShapeDtypeStruct(a.shape, F32),
        in_specs=[IN_VMEM] * 2,
        out_specs=IN_VMEM,
        compiler_params=pltpu.CompilerParams(vmem_limit_bytes=4 * MIB),
        cost_estimate=pl.CostEstimate(flops=1 << 34, bytes_accessed=32 * MIB, transcendentals=0),
    )(a, b)


def final_kernel(kept, up_own, from_x, other, m_y, m_xy, out):
    _, z_low, y, _, _ = place()
    line = pl.ds(out.shape[0], RANK)
    parts = [m_y[pl.ds(i * RANK, RANK), :].astype(F32) for i in range(3)]
    m = (kept[line, :] + from_x[line, :]) + ((parts[0] + parts[1]) + parts[2] + m_xy[...])
    mid = m.T.astype(BF16)
    up = []
    for b in range(2):
        for i in range(UP_TILES):
            lines = pl.ds((b * 2 + i // 2 + 3) * RANK, RANK)
            got = m_y[lines, pl.ds(i % 2 * LANES, LANES)]
            up.append(up_own[b, :, pl.ds(i * LANES, LANES)] + got)
    for tile in range(2):
        cols = pl.ds(tile * LANES, LANES)
        for side in range(2):
            j = 2 * (z_low ^ tile) + (y ^ side)
            lanes = pl.ds(pl.multiple_of(j * LANES, LANES), LANES)
            for b in range(2):
                span = pl.ds(b * BLK, BLK)
                if side == 0:
                    base = kept[span, cols] + from_x[span, cols]
                else:
                    base = other[span, cols]
                picked = jnp.zeros((RANK, LANES), BF16)
                for i in range(UP_TILES):
                    picked = jnp.where(j == i, up[b * UP_TILES + i], picked)
                extra = jnp.dot(
                    mid[b * BLK : (b + 1) * BLK], picked, preferred_element_type=F32
                )
                out[span, lanes] = (base + extra).astype(BF16)


def final(*args):
    rows = args[0].shape[0] - RANK
    return pl.pallas_call(
        final_kernel,
        out_shape=jax.ShapeDtypeStruct((rows, 2 * HALF), BF16),
        in_specs=[IN_VMEM] * len(args),
        out_specs=IN_VMEM,
        compiler_params=pltpu.CompilerParams(vmem_limit_bytes=6 * MIB),
    )(*args)


def make_body(tensor, adapters):
    over_tensor, over_adapter = swaps(tensor, adapters)
    tie = lax.optimization_barrier

    def over_both(array):
        pairs = [
            (i * adapters + j, (i ^ 2) * adapters + (j ^ 1))
            for i in range(tensor)
            for j in range(adapters)
        ]
        return lax.ppermute(array, ("tensor", "adapter"), perm=pairs)

    def body(hidden, value, down, up, chosen, live):
        features = hidden.shape[1]
        w0, down = value.T, down.transpose(0, 2, 1).reshape(RANK, features)
        theirs = over_tensor(hidden, 2)
        w2, w1 = over_tensor(w0, 8), over_tensor(w0, 4)
        half = lax.dynamic_slice_in_dim(up[0], lax.axis_index("adapter") * 2 * HALF, 2 * HALF, 1)
        d0 = jnp.concatenate([down, half], axis=1)
        ids = jnp.concatenate([chosen, live])
        w2, w0, d0 = tie((w2, w0, d0))
        w3 = over_tensor(w2, 4)
        d2, d1 = over_tensor(d0, 8), over_tensor(d0, 4)
        w = jnp.concatenate([w0, w1, w2])
        v = over_tensor(w, 1)
        d3 = over_tensor(d0, 12)
        d1, d2, d3, w3, ids = tie((d1, d2, d3, w3, ids))
        v3, ids_p = over_tensor(w3, 1), over_tensor(ids, 2)
        narrow = jnp.concatenate([d0, d1, d2, d3])
        narrow_v = over_tensor(narrow, 1)
        wide = (w, w3, v, v3)
        to_y, to_xy = base_sums(theirs, wide)
        to_y, to_xy, ids_p = tie((to_y, to_xy, ids_p))
        other = add(over_tensor(to_y, 2), over_both(to_xy))
        narrow = (narrow, narrow_v)
        kept, to_x, m_y, m_xy, up_own = own_sums(
            (ids, ids_p), hidden, theirs, narrow, wide
        )
        from_x, m_y, m_xy = over_adapter(to_x, 1), over_tensor(m_y, 2), over_both(m_xy)
        return final(kept, up_own, from_x, other, m_y, m_xy)

    return body


def solution(mesh):
    in_specs = (
        P(("groups", "tensor"), "adapter"),
        P("adapter", "tensor"),
        P("tensor", "adapter", None),
        P("tensor", None, None),
        P(("groups", "tensor")),
        P(("groups", "tensor")),
    )
    out_specs = P(("groups", "tensor"), "adapter")
    tensor, adapters = mesh.shape["tensor"], mesh.shape["adapter"]

    def run(hidden, value, down, up, chosen, live):
        blocks = chosen.shape[0] // (mesh.shape["groups"] * tensor)
        fits = (tensor, adapters, blocks) == (4 * DEPTH, 2, 2)
        fits = fits and up.shape == (tensor, RANK, tensor * WIDTH)
        make = make_body if fits else make_general_body
        body = make(tensor, adapters)
        mapped = jax.shard_map(
            body, mesh=mesh, in_specs=in_specs, out_specs=out_specs, check_vma=False
        )
        return mapped(hidden, value, down, up, chosen, live)

    return run
```

```python
import jax
import jax.numpy as jnp
from jax import lax
from jax.experimental import pallas as pl
from jax.experimental.pallas import tpu as pltpu
from jax.sharding import PartitionSpec as P

BLK = 128
LANES = 128
F32 = jnp.float32
BF16 = jnp.bfloat16
MIB = 1 << 20


def dot_nt(a, b):
    return lax.dot_general(a, b, (((1,), (1,)), ((), ())), preferred_element_type=F32)


def swaps(tensor, adapters):
    def over_tensor(array, flip):
        return lax.ppermute(array, "tensor", perm=[(i, i ^ flip) for i in range(tensor)])

    def over_adapter(array, flip):
        return lax.ppermute(array, "adapter", perm=[(i, i ^ flip) for i in range(adapters)])

    return over_tensor, over_adapter


def make_general_body(tensor, adapters):
    depth = tensor // 4
    low = depth // adapters
    over_tensor, over_adapter = swaps(tensor, adapters)

    def body(hidden, value, down, up, chosen, live):
        t, x = lax.axis_index("tensor"), lax.axis_index("adapter")
        z, y, core = t // 4, (t // 2) % 2, t % 2
        rows, features = hidden.shape
        width = value.shape[1]
        homes, rank, wide = up.shape
        blocks = rows // BLK

        theirs = over_tensor(hidden, 2)
        packet = jnp.concatenate([value.T, down.transpose(0, 2, 1).reshape(homes * rank, features)])
        units = {0: packet}
        bit = depth // 2
        while bit:
            units.update({a ^ bit: over_tensor(u, 4 * bit) for a, u in units.items()})
            bit //= 2
        pairs = {a: (u, over_tensor(u, 1)) for a, u in units.items()}

        ids = jnp.stack([chosen, live])
        ids = jnp.concatenate([ids, over_tensor(ids, 2)], axis=1)
        ups = lax.dynamic_slice_in_dim(up, x * (wide // adapters), wide // adapters, 2)[None]
        bit = 1
        while bit < tensor:
            ups = jnp.concatenate([ups, over_tensor(ups, bit)])
            bit *= 2

        w_all = jnp.concatenate([u[:width] for a in range(depth) for u in pairs[a]])
        d_all = jnp.concatenate([u[width:] for a in range(depth) for u in pairs[a]])

        relative = (ids[0] // homes) ^ t
        here = (relative & 2) == 0
        slot = (relative // 4) * 2 + relative % 2
        which = slot * homes + ids[0] % homes

        ups = ups.reshape(tensor, homes, rank, low, 2, 2, width)
        ups = lax.dynamic_index_in_dim(ups, y, 4, keepdims=False)
        z_low = z % low
        order = [lax.dynamic_index_in_dim(ups, z_low ^ a, 3, keepdims=False) for a in range(low)]
        ups = jnp.stack(order, axis=3)
        ups = jnp.where(core == 1, ups[..., ::-1, :], ups)
        ups = ups.reshape(tensor * homes, rank, low * 2 * width)
        up_index = relative * homes + ids[0] % homes

        part = (z // low) ^ x

        def work(x_rows, b0):
            count = x_rows.shape[0] // BLK
            base = dot_nt(x_rows, w_all).reshape(-1, adapters, low * 2 * width)
            kept = lax.dynamic_index_in_dim(base, part, 1, keepdims=False)
            for k in range(1, adapters):
                sent = lax.dynamic_index_in_dim(base, part ^ k, 1, keepdims=False)
                kept = kept + over_adapter(sent, k)
            shrink = dot_nt(x_rows, d_all).reshape(count, BLK, -1, rank)
            spots = jnp.arange(shrink.shape[2], dtype=jnp.int32)
            hot = (which[b0 : b0 + count, None] == spots) & here[b0 : b0 + count, None]
            alive = jnp.arange(BLK, dtype=jnp.int32) < ids[1, b0 : b0 + count, None]
            mask = hot[:, None, :, None] & alive[:, :, None, None]
            return kept, jnp.where(mask, shrink, 0.0).sum(axis=2)

        def finish(kept, shrink, b0):
            mid = shrink.astype(BF16)
            picked = [
                lax.dynamic_index_in_dim(ups, up_index[b], 0, keepdims=False)
                for b in range(b0, b0 + shrink.shape[0])
            ]
            extra = jnp.einsum("bir,brv->biv", mid, jnp.stack(picked), preferred_element_type=F32)
            return (kept + extra.reshape(kept.shape)).astype(BF16)

        kept_own, m_own = work(hidden, 0)
        kept_their, m_their = work(theirs, blocks)
        m = jnp.concatenate([m_own, m_their])
        total = m
        for k in range(1, adapters):
            total = total + over_adapter(m, k)
        m = total.astype(BF16)
        swapped = over_tensor(m, 2)
        m = m + jnp.concatenate([swapped[blocks:], swapped[:blocks]])
        out_their = over_tensor(finish(kept_their, m[blocks:], blocks), 2)
        out_own = finish(kept_own, m[:blocks], 0)
        pair = jnp.stack([out_own, out_their], axis=1)
        pair = pair.reshape(rows, 2, low, 2, width)
        pair = jnp.where(y == 1, pair[:, ::-1], pair)
        pair = jnp.where(core == 1, pair[:, :, :, ::-1], pair)
        pair = jnp.stack(
            [lax.dynamic_index_in_dim(pair, z_low ^ a, 2, keepdims=False) for a in range(low)],
            axis=1,
        )
        return pair.reshape(rows, wide // adapters)

    return body


RANK = 16
WIDTH = 64
DEPTH = 4
TILE = 2 * WIDTH
HALF = 2 * TILE
UP_TILES = 4
VMEM = 16 * MIB
IN_SMEM = pl.BlockSpec(memory_space=pltpu.SMEM)
IN_VMEM = pl.BlockSpec(memory_space=pltpu.VMEM)
IN_HBM = pl.BlockSpec(memory_space=pltpu.HBM)
IN_ANY = pl.BlockSpec(memory_space=pl.ANY)


def place():
    t = lax.axis_index("tensor")
    z, y, core = t // 4, (t // 2) % 2, t % 2
    part = (z // 2) ^ lax.axis_index("adapter")
    return t, z % 2, y, core, part


def gather_wide(wide, w, sems):
    _, _, _, core, part = place()
    copies = []
    for a in range(DEPTH):
        base = ((a // 2) ^ part) * HALF + (a % 2) * TILE
        last = a == DEPTH - 1
        for k in range(2):
            start = pl.multiple_of(base + (core ^ k) * WIDTH, WIDTH)
            copies.append(
                pltpu.make_async_copy(
                    wide[2 * k + last].at[pl.ds(0 if last else a * WIDTH, WIDTH)],
                    w.at[pl.ds(start, WIDTH), :],
                    sems.at[2 * a + k],
                )
            )
    for c in copies:
        c.start()
    return copies


def base_kernel(rows_in, *refs):
    wide, (kept, sent, w, w_sem) = refs[:4], refs[4:]
    copies = gather_wide(wide, w, w_sem)
    for c in copies:
        c.wait()
    sent[...] = dot_nt(rows_in[...], w[pl.ds(HALF, HALF), :])
    kept[...] = dot_nt(rows_in[...], w[pl.ds(0, HALF), :])


def base_sums(rows_in, wide):
    rows, features = rows_in.shape
    return pl.pallas_call(
        base_kernel,
        out_shape=[jax.ShapeDtypeStruct((rows, HALF), F32)] * 2,
        in_specs=[IN_VMEM] + [IN_ANY] * len(wide),
        out_specs=[IN_VMEM] * 2,
        scratch_shapes=[
            pltpu.VMEM((2 * HALF, features), BF16),
            pltpu.SemaphoreType.DMA((2 * DEPTH,)),
        ],
        compiler_params=pltpu.CompilerParams(vmem_limit_bytes=9 * MIB),
        cost_estimate=pl.CostEstimate(flops=0, bytes_accessed=0, transcendentals=0),
    )(rows_in, *wide)


def own_kernel(ids, ids_p, mine, theirs, *refs):
    wide, narrow, refs = refs[:4], refs[4:6], refs[6:]
    kept, to_x, m_y, m_xy, up_own, w, d, up, w_sem, d_sem = refs
    t = lax.axis_index("tensor")
    rows, features = mine.shape
    cols = pl.ds(0, features)
    copies = gather_wide(wide, w, w_sem)

    def fetch(b, ref, line):
        lines = pl.ds(line, RANK)
        return [
            pltpu.make_async_copy(ref.at[lines, cols], d.at[b], d_sem.at[2 * b]),
            pltpu.make_async_copy(
                ref.at[lines, pl.ds(features, 2 * HALF)], up.at[b], d_sem.at[2 * b + 1]
            ),
        ]

    where = []
    for b in range(4):
        relative = (ids[b] if b < 2 else ids_p[b - 2]) ^ t
        here = ((relative // 2) % 2) == 0
        unit, other = relative // 4, relative % 2
        where.append(here)

        @pl.when(jnp.logical_not(here))
        def _():
            d[b] = jnp.zeros_like(d[b])
            up[b] = jnp.zeros_like(up[b])

        for i, ref in enumerate(narrow):

            @pl.when(here & (other == i))
            def _():
                for c in fetch(b, ref, pl.multiple_of(unit * RANK, RANK)):
                    c.start()

    for c in copies:
        c.wait()
    to_x[:rows, :] = dot_nt(mine[...], w[pl.ds(HALF, HALF), :])
    kept[:rows, :] = dot_nt(mine[...], w[pl.ds(0, HALF), :])
    for b, here in enumerate(where):

        @pl.when(here)
        def _():
            for c in fetch(b, narrow[0], 0):
                c.wait()

    for b in range(4):
        at = pl.ds(b % 2 * BLK, BLK)
        m = dot_nt(d[b], (mine if b < 2 else theirs)[at, :])
        limit = ids[2 + b] if b < 2 else ids_p[b]
        m = jnp.where(lax.broadcasted_iota(jnp.int32, m.shape, 1) < limit, m, 0.0)
        if b < 2:
            kept[pl.ds(rows, RANK), at] = m
            to_x[pl.ds(rows, RANK), at] = m
            up_own[b] = up[b]
        else:
            m_xy[:, at] = m
            for i in range(3):
                part = m.astype(BF16)
                m_y[pl.ds(i * RANK, RANK), at] = part
                m = m - part.astype(F32)
            for i in range(2):
                m_y[pl.ds((b % 2 * 2 + i + 3) * RANK, RANK), :] = up[b, :, pl.ds(i * HALF, HALF)]


def own_sums(scalars, mine, theirs, narrow, wide):
    rows, features = mine.shape
    part, m_xy = ((rows + RANK, HALF), F32), ((RANK, HALF), F32)
    shapes = [part, part, ((7 * RANK, HALF), BF16), m_xy, ((2, RANK, 2 * HALF), BF16)]
    return pl.pallas_call(
        own_kernel,
        out_shape=[jax.ShapeDtypeStruct(*s) for s in shapes],
        in_specs=[IN_SMEM] * 2 + [IN_VMEM] * 2 + [IN_ANY] * (len(wide) + len(narrow)),
        out_specs=[IN_VMEM] * 5,
        scratch_shapes=[
            pltpu.VMEM((2 * HALF, features), BF16),
            pltpu.VMEM((4, RANK, features), BF16),
            pltpu.VMEM((4, RANK, 2 * HALF), BF16),
            pltpu.SemaphoreType.DMA((2 * DEPTH,)),
            pltpu.SemaphoreType.DMA((8,)),
        ],
        compiler_params=pltpu.CompilerParams(vmem_limit_bytes=9 * MIB),
        cost_estimate=pl.CostEstimate(flops=0, bytes_accessed=0, transcendentals=0),
    )(*scalars, mine, theirs, *wide, *narrow)


def add_kernel(a, b, out):
    out[...] = a[...] + b[...]


def add(a, b):
    return pl.pallas_call(
        add_kernel,
        out_shape=jax.ShapeDtypeStruct(a.shape, F32),
        in_specs=[IN_VMEM] * 2,
        out_specs=IN_VMEM,
        compiler_params=pltpu.CompilerParams(vmem_limit_bytes=4 * MIB),
        cost_estimate=pl.CostEstimate(flops=1 << 34, bytes_accessed=32 * MIB, transcendentals=0),
    )(a, b)


def final_kernel(kept, up_own, from_x, other, m_y, m_xy, out):
    _, z_low, y, _, _ = place()
    line = pl.ds(out.shape[0], RANK)
    parts = [m_y[pl.ds(i * RANK, RANK), :].astype(F32) for i in range(3)]
    m = (kept[line, :] + from_x[line, :]) + ((parts[0] + parts[1]) + parts[2] + m_xy[...])
    mid = m.T.astype(BF16)
    up = []
    for b in range(2):
        for i in range(UP_TILES):
            lines = pl.ds((b * 2 + i // 2 + 3) * RANK, RANK)
            got = m_y[lines, pl.ds(i % 2 * LANES, LANES)]
            up.append(up_own[b, :, pl.ds(i * LANES, LANES)] + got)
    for tile in range(2):
        cols = pl.ds(tile * LANES, LANES)
        for side in range(2):
            j = 2 * (z_low ^ tile) + (y ^ side)
            lanes = pl.ds(pl.multiple_of(j * LANES, LANES), LANES)
            for b in range(2):
                span = pl.ds(b * BLK, BLK)
                if side == 0:
                    base = kept[span, cols] + from_x[span, cols]
                else:
                    base = other[span, cols]
                picked = jnp.zeros((RANK, LANES), BF16)
                for i in range(UP_TILES):
                    picked = jnp.where(j == i, up[b * UP_TILES + i], picked)
                extra = jnp.dot(
                    mid[b * BLK : (b + 1) * BLK], picked, preferred_element_type=F32
                )
                out[span, lanes] = (base + extra).astype(BF16)


def final(*args):
    rows = args[0].shape[0] - RANK
    return pl.pallas_call(
        final_kernel,
        out_shape=jax.ShapeDtypeStruct((rows, 2 * HALF), BF16),
        in_specs=[IN_VMEM] * len(args),
        out_specs=IN_VMEM,
        compiler_params=pltpu.CompilerParams(vmem_limit_bytes=6 * MIB),
    )(*args)


def make_body(tensor, adapters):
    over_tensor, over_adapter = swaps(tensor, adapters)
    tie = lax.optimization_barrier

    def over_both(array):
        pairs = [
            (i * adapters + j, (i ^ 2) * adapters + (j ^ 1))
            for i in range(tensor)
            for j in range(adapters)
        ]
        return lax.ppermute(array, ("tensor", "adapter"), perm=pairs)

    def body(hidden, value, down, up, chosen, live):
        features = hidden.shape[1]
        w0, down = value.T, down.transpose(0, 2, 1).reshape(RANK, features)
        theirs = over_tensor(hidden, 2)
        w2, w1 = over_tensor(w0, 8), over_tensor(w0, 4)
        half = lax.dynamic_slice_in_dim(up[0], lax.axis_index("adapter") * 2 * HALF, 2 * HALF, 1)
        d0 = jnp.concatenate([down, half], axis=1)
        ids = jnp.concatenate([chosen, live])
        w2, w0, d0 = tie((w2, w0, d0))
        w3 = over_tensor(w2, 4)
        d2, d1 = over_tensor(d0, 8), over_tensor(d0, 4)
        w = jnp.concatenate([w0, w1, w2])
        v = over_tensor(w, 1)
        d3 = over_tensor(d0, 12)
        d1, d2, d3, w3, ids = tie((d1, d2, d3, w3, ids))
        v3, ids_p = over_tensor(w3, 1), over_tensor(ids, 2)
        narrow = jnp.concatenate([d0, d1, d2, d3])
        narrow_v = over_tensor(narrow, 1)
        wide = (w, w3, v, v3)
        to_y, to_xy = base_sums(theirs, wide)
        to_y, to_xy, ids_p = tie((to_y, to_xy, ids_p))
        other = add(over_both(to_xy), over_tensor(to_y, 2))
        narrow = (narrow, narrow_v)
        kept, to_x, m_y, m_xy, up_own = own_sums(
            (ids, ids_p), hidden, theirs, narrow, wide
        )
        from_x, m_y, m_xy = over_adapter(to_x, 1), over_tensor(m_y, 2), over_both(m_xy)
        return final(kept, up_own, from_x, other, m_y, m_xy)

    return body


def solution(mesh):
    in_specs = (
        P(("groups", "tensor"), "adapter"),
        P("adapter", "tensor"),
        P("tensor", "adapter", None),
        P("tensor", None, None),
        P(("groups", "tensor")),
        P(("groups", "tensor")),
    )
    out_specs = P(("groups", "tensor"), "adapter")
    tensor, adapters = mesh.shape["tensor"], mesh.shape["adapter"]

    def run(hidden, value, down, up, chosen, live):
        blocks = chosen.shape[0] // (mesh.shape["groups"] * tensor)
        fits = (tensor, adapters, blocks) == (4 * DEPTH, 2, 2)
        fits = fits and up.shape == (tensor, RANK, tensor * WIDTH)
        make = make_body if fits else make_general_body
        body = make(tensor, adapters)
        mapped = jax.shard_map(
            body, mesh=mesh, in_specs=in_specs, out_specs=out_specs, check_vma=False
        )
        return mapped(hidden, value, down, up, chosen, live)

    return run
```

```python
import jax
import jax.numpy as jnp
from jax import lax
from jax.experimental import pallas as pl
from jax.experimental.pallas import tpu as pltpu
from jax.sharding import PartitionSpec as P

BLK = 128
LANES = 128
F32 = jnp.float32
BF16 = jnp.bfloat16
MIB = 1 << 20


def dot_nt(a, b):
    return lax.dot_general(a, b, (((1,), (1,)), ((), ())), preferred_element_type=F32)


def swaps(tensor, adapters):
    def over_tensor(array, flip):
        return lax.ppermute(array, "tensor", perm=[(i, i ^ flip) for i in range(tensor)])

    def over_adapter(array, flip):
        return lax.ppermute(array, "adapter", perm=[(i, i ^ flip) for i in range(adapters)])

    return over_tensor, over_adapter


def make_general_body(tensor, adapters):
    depth = tensor // 4
    low = depth // adapters
    over_tensor, over_adapter = swaps(tensor, adapters)

    def body(hidden, value, down, up, chosen, live):
        t, x = lax.axis_index("tensor"), lax.axis_index("adapter")
        z, y, core = t // 4, (t // 2) % 2, t % 2
        rows, features = hidden.shape
        width = value.shape[1]
        homes, rank, wide = up.shape
        blocks = rows // BLK

        theirs = over_tensor(hidden, 2)
        packet = jnp.concatenate([value.T, down.transpose(0, 2, 1).reshape(homes * rank, features)])
        units = {0: packet}
        bit = depth // 2
        while bit:
            units.update({a ^ bit: over_tensor(u, 4 * bit) for a, u in units.items()})
            bit //= 2
        pairs = {a: (u, over_tensor(u, 1)) for a, u in units.items()}

        ids = jnp.stack([chosen, live])
        ids = jnp.concatenate([ids, over_tensor(ids, 2)], axis=1)
        ups = lax.dynamic_slice_in_dim(up, x * (wide // adapters), wide // adapters, 2)[None]
        bit = 1
        while bit < tensor:
            ups = jnp.concatenate([ups, over_tensor(ups, bit)])
            bit *= 2

        w_all = jnp.concatenate([u[:width] for a in range(depth) for u in pairs[a]])
        d_all = jnp.concatenate([u[width:] for a in range(depth) for u in pairs[a]])

        relative = (ids[0] // homes) ^ t
        here = (relative & 2) == 0
        slot = (relative // 4) * 2 + relative % 2
        which = slot * homes + ids[0] % homes

        ups = ups.reshape(tensor, homes, rank, low, 2, 2, width)
        ups = lax.dynamic_index_in_dim(ups, y, 4, keepdims=False)
        z_low = z % low
        order = [lax.dynamic_index_in_dim(ups, z_low ^ a, 3, keepdims=False) for a in range(low)]
        ups = jnp.stack(order, axis=3)
        ups = jnp.where(core == 1, ups[..., ::-1, :], ups)
        ups = ups.reshape(tensor * homes, rank, low * 2 * width)
        up_index = relative * homes + ids[0] % homes

        part = (z // low) ^ x

        def work(x_rows, b0):
            count = x_rows.shape[0] // BLK
            base = dot_nt(x_rows, w_all).reshape(-1, adapters, low * 2 * width)
            kept = lax.dynamic_index_in_dim(base, part, 1, keepdims=False)
            for k in range(1, adapters):
                sent = lax.dynamic_index_in_dim(base, part ^ k, 1, keepdims=False)
                kept = kept + over_adapter(sent, k)
            shrink = dot_nt(x_rows, d_all).reshape(count, BLK, -1, rank)
            spots = jnp.arange(shrink.shape[2], dtype=jnp.int32)
            hot = (which[b0 : b0 + count, None] == spots) & here[b0 : b0 + count, None]
            alive = jnp.arange(BLK, dtype=jnp.int32) < ids[1, b0 : b0 + count, None]
            mask = hot[:, None, :, None] & alive[:, :, None, None]
            return kept, jnp.where(mask, shrink, 0.0).sum(axis=2)

        def finish(kept, shrink, b0):
            mid = shrink.astype(BF16)
            picked = [
                lax.dynamic_index_in_dim(ups, up_index[b], 0, keepdims=False)
                for b in range(b0, b0 + shrink.shape[0])
            ]
            extra = jnp.einsum("bir,brv->biv", mid, jnp.stack(picked), preferred_element_type=F32)
            return (kept + extra.reshape(kept.shape)).astype(BF16)

        kept_own, m_own = work(hidden, 0)
        kept_their, m_their = work(theirs, blocks)
        m = jnp.concatenate([m_own, m_their])
        total = m
        for k in range(1, adapters):
            total = total + over_adapter(m, k)
        m = total.astype(BF16)
        swapped = over_tensor(m, 2)
        m = m + jnp.concatenate([swapped[blocks:], swapped[:blocks]])
        out_their = over_tensor(finish(kept_their, m[blocks:], blocks), 2)
        out_own = finish(kept_own, m[:blocks], 0)
        pair = jnp.stack([out_own, out_their], axis=1)
        pair = pair.reshape(rows, 2, low, 2, width)
        pair = jnp.where(y == 1, pair[:, ::-1], pair)
        pair = jnp.where(core == 1, pair[:, :, :, ::-1], pair)
        pair = jnp.stack(
            [lax.dynamic_index_in_dim(pair, z_low ^ a, 2, keepdims=False) for a in range(low)],
            axis=1,
        )
        return pair.reshape(rows, wide // adapters)

    return body


RANK = 16
WIDTH = 64
DEPTH = 4
TILE = 2 * WIDTH
HALF = 2 * TILE
UP_TILES = 4
VMEM = 16 * MIB
IN_SMEM = pl.BlockSpec(memory_space=pltpu.SMEM)
IN_VMEM = pl.BlockSpec(memory_space=pltpu.VMEM)
IN_HBM = pl.BlockSpec(memory_space=pltpu.HBM)
IN_ANY = pl.BlockSpec(memory_space=pl.ANY)


def place():
    t = lax.axis_index("tensor")
    z, y, core = t // 4, (t // 2) % 2, t % 2
    part = (z // 2) ^ lax.axis_index("adapter")
    return t, z % 2, y, core, part


def gather_wide(wide, w, sems):
    _, _, _, core, part = place()
    copies = []
    for a in range(DEPTH):
        base = ((a // 2) ^ part) * HALF + (a % 2) * TILE
        last = a == DEPTH - 1
        for k in range(2):
            start = pl.multiple_of(base + (core ^ k) * WIDTH, WIDTH)
            copies.append(
                pltpu.make_async_copy(
                    wide[2 * k + last].at[pl.ds(0 if last else a * WIDTH, WIDTH)],
                    w.at[pl.ds(start, WIDTH), :],
                    sems.at[2 * a + k],
                )
            )
    for c in copies:
        c.start()
    return copies


def base_kernel(rows_in, *refs):
    wide, (kept, sent, w, w_sem) = refs[:4], refs[4:]
    copies = gather_wide(wide, w, w_sem)
    for c in copies:
        c.wait()
    sent[...] = dot_nt(rows_in[...], w[pl.ds(HALF, HALF), :])
    kept[...] = dot_nt(rows_in[...], w[pl.ds(0, HALF), :])


def base_sums(rows_in, wide):
    rows, features = rows_in.shape
    return pl.pallas_call(
        base_kernel,
        out_shape=[jax.ShapeDtypeStruct((rows, HALF), F32)] * 2,
        in_specs=[IN_VMEM] + [IN_ANY] * len(wide),
        out_specs=[IN_VMEM] * 2,
        scratch_shapes=[
            pltpu.VMEM((2 * HALF, features), BF16),
            pltpu.SemaphoreType.DMA((2 * DEPTH,)),
        ],
        compiler_params=pltpu.CompilerParams(vmem_limit_bytes=9 * MIB),
        cost_estimate=pl.CostEstimate(flops=0, bytes_accessed=0, transcendentals=0),
    )(rows_in, *wide)


def own_kernel(ids, ids_p, mine, theirs, *refs):
    wide, narrow, refs = refs[:4], refs[4:6], refs[6:]
    kept, to_x, m_y, m_xy, up_own, w, d, up, w_sem, d_sem = refs
    t = lax.axis_index("tensor")
    rows, features = mine.shape
    cols = pl.ds(0, features)
    copies = gather_wide(wide, w, w_sem)

    def fetch(b, ref, line):
        lines = pl.ds(line, RANK)
        return [
            pltpu.make_async_copy(ref.at[lines, cols], d.at[b], d_sem.at[2 * b]),
            pltpu.make_async_copy(
                ref.at[lines, pl.ds(features, 2 * HALF)], up.at[b], d_sem.at[2 * b + 1]
            ),
        ]

    where = []
    for b in range(4):
        relative = (ids[b] if b < 2 else ids_p[b - 2]) ^ t
        here = ((relative // 2) % 2) == 0
        unit, other = relative // 4, relative % 2
        where.append(here)

        @pl.when(jnp.logical_not(here))
        def _():
            d[b] = jnp.zeros_like(d[b])
            up[b] = jnp.zeros_like(up[b])

        for i, ref in enumerate(narrow):

            @pl.when(here & (other == i))
            def _():
                for c in fetch(b, ref, pl.multiple_of(unit * RANK, RANK)):
                    c.start()

    for c in copies:
        c.wait()
    to_x[:rows, :] = dot_nt(mine[...], w[pl.ds(HALF, HALF), :])
    kept[:rows, :] = dot_nt(mine[...], w[pl.ds(0, HALF), :])
    for b, here in enumerate(where):

        @pl.when(here)
        def _():
            for c in fetch(b, narrow[0], 0):
                c.wait()

    for b in range(4):
        at = pl.ds(b % 2 * BLK, BLK)
        m = dot_nt(d[b], (mine if b < 2 else theirs)[at, :])
        limit = ids[2 + b] if b < 2 else ids_p[b]
        m = jnp.where(lax.broadcasted_iota(jnp.int32, m.shape, 1) < limit, m, 0.0)
        if b < 2:
            kept[pl.ds(rows, RANK), at] = m
            to_x[pl.ds(rows, RANK), at] = m
            up_own[b] = up[b]
        else:
            m_xy[:, at] = m
            for i in range(3):
                part = m.astype(BF16)
                m_y[pl.ds(i * RANK, RANK), at] = part
                m = m - part.astype(F32)
            for i in range(2):
                m_y[pl.ds((b % 2 * 2 + i + 3) * RANK, RANK), :] = up[b, :, pl.ds(i * HALF, HALF)]


def own_sums(scalars, mine, theirs, narrow, wide):
    rows, features = mine.shape
    part, m_xy = ((rows + RANK, HALF), F32), ((RANK, HALF), F32)
    shapes = [part, part, ((7 * RANK, HALF), BF16), m_xy, ((2, RANK, 2 * HALF), BF16)]
    return pl.pallas_call(
        own_kernel,
        out_shape=[jax.ShapeDtypeStruct(*s) for s in shapes],
        in_specs=[IN_SMEM] * 2 + [IN_VMEM] * 2 + [IN_ANY] * (len(wide) + len(narrow)),
        out_specs=[IN_VMEM] * 5,
        scratch_shapes=[
            pltpu.VMEM((2 * HALF, features), BF16),
            pltpu.VMEM((4, RANK, features), BF16),
            pltpu.VMEM((4, RANK, 2 * HALF), BF16),
            pltpu.SemaphoreType.DMA((2 * DEPTH,)),
            pltpu.SemaphoreType.DMA((8,)),
        ],
        compiler_params=pltpu.CompilerParams(vmem_limit_bytes=9 * MIB),
        cost_estimate=pl.CostEstimate(flops=0, bytes_accessed=0, transcendentals=0),
    )(*scalars, mine, theirs, *wide, *narrow)


def add_kernel(a, b, out):
    out[...] = a[...] + b[...]


def add(a, b):
    return pl.pallas_call(
        add_kernel,
        out_shape=jax.ShapeDtypeStruct(a.shape, F32),
        in_specs=[IN_VMEM] * 2,
        out_specs=IN_VMEM,
        compiler_params=pltpu.CompilerParams(vmem_limit_bytes=4 * MIB),
        cost_estimate=pl.CostEstimate(flops=1 << 34, bytes_accessed=32 * MIB, transcendentals=0),
    )(a, b)


def final_kernel(kept, up_own, from_x, other, m_y, m_xy, out):
    _, z_low, y, _, _ = place()
    line = pl.ds(out.shape[0], RANK)
    parts = [m_y[pl.ds(i * RANK, RANK), :].astype(F32) for i in range(3)]
    m = (kept[line, :] + from_x[line, :]) + ((parts[0] + parts[1]) + parts[2] + m_xy[...])
    mid = m.T.astype(BF16)
    up = []
    for b in range(2):
        for i in range(UP_TILES):
            lines = pl.ds((b * 2 + i // 2 + 3) * RANK, RANK)
            got = m_y[lines, pl.ds(i % 2 * LANES, LANES)]
            up.append(up_own[b, :, pl.ds(i * LANES, LANES)] + got)
    for tile in range(2):
        cols = pl.ds(tile * LANES, LANES)
        for side in range(2):
            j = 2 * (z_low ^ tile) + (y ^ side)
            lanes = pl.ds(pl.multiple_of(j * LANES, LANES), LANES)
            for b in range(2):
                span = pl.ds(b * BLK, BLK)
                if side == 0:
                    base = kept[span, cols] + from_x[span, cols]
                else:
                    base = other[span, cols]
                picked = jnp.zeros((RANK, LANES), BF16)
                for i in range(UP_TILES):
                    picked = jnp.where(j == i, up[b * UP_TILES + i], picked)
                extra = jnp.dot(
                    mid[b * BLK : (b + 1) * BLK], picked, preferred_element_type=F32
                )
                out[span, lanes] = (base + extra).astype(BF16)


def final(*args):
    rows = args[0].shape[0] - RANK
    return pl.pallas_call(
        final_kernel,
        out_shape=jax.ShapeDtypeStruct((rows, 2 * HALF), BF16),
        in_specs=[IN_VMEM] * len(args),
        out_specs=IN_VMEM,
        compiler_params=pltpu.CompilerParams(vmem_limit_bytes=6 * MIB),
    )(*args)


def make_body(tensor, adapters):
    over_tensor, over_adapter = swaps(tensor, adapters)
    tie = lax.optimization_barrier

    def over_both(array):
        pairs = [
            (i * adapters + j, (i ^ 2) * adapters + (j ^ 1))
            for i in range(tensor)
            for j in range(adapters)
        ]
        return lax.ppermute(array, ("tensor", "adapter"), perm=pairs)

    def body(hidden, value, down, up, chosen, live):
        features = hidden.shape[1]
        w0, down = value.T, down.transpose(0, 2, 1).reshape(RANK, features)
        theirs = over_tensor(hidden, 2)
        w2, w1 = over_tensor(w0, 8), over_tensor(w0, 4)
        half = lax.dynamic_slice_in_dim(up[0], lax.axis_index("adapter") * 2 * HALF, 2 * HALF, 1)
        d0 = jnp.concatenate([down, half], axis=1)
        ids = jnp.concatenate([chosen, live])
        w2, w0, d0 = tie((w2, w0, d0))
        w3 = over_tensor(w2, 4)
        d2, d1 = over_tensor(d0, 8), over_tensor(d0, 4)
        w = jnp.concatenate([w0, w1, w2])
        v = over_tensor(w, 1)
        d3 = over_tensor(d0, 12)
        d1, d2, d3, w3 = tie((d1, d2, d3, w3))
        v3, ids_p = over_tensor(w3, 1), over_tensor(ids, 2)
        narrow = jnp.concatenate([d0, d1, d2, d3])
        narrow_v = over_tensor(narrow, 1)
        wide = (w, w3, v, v3)
        to_y, to_xy = base_sums(theirs, wide)
        to_y, to_xy, ids_p = tie((to_y, to_xy, ids_p))
        other = add(over_both(to_xy), over_tensor(to_y, 2))
        narrow = (narrow, narrow_v)
        kept, to_x, m_y, m_xy, up_own = own_sums(
            (ids, ids_p), hidden, theirs, narrow, wide
        )
        from_x, m_y, m_xy = over_adapter(to_x, 1), over_tensor(m_y, 2), over_both(m_xy)
        return final(kept, up_own, from_x, other, m_y, m_xy)

    return body


def solution(mesh):
    in_specs = (
        P(("groups", "tensor"), "adapter"),
        P("adapter", "tensor"),
        P("tensor", "adapter", None),
        P("tensor", None, None),
        P(("groups", "tensor")),
        P(("groups", "tensor")),
    )
    out_specs = P(("groups", "tensor"), "adapter")
    tensor, adapters = mesh.shape["tensor"], mesh.shape["adapter"]

    def run(hidden, value, down, up, chosen, live):
        blocks = chosen.shape[0] // (mesh.shape["groups"] * tensor)
        fits = (tensor, adapters, blocks) == (4 * DEPTH, 2, 2)
        fits = fits and up.shape == (tensor, RANK, tensor * WIDTH)
        make = make_body if fits else make_general_body
        body = make(tensor, adapters)
        mapped = jax.shard_map(
            body, mesh=mesh, in_specs=in_specs, out_specs=out_specs, check_vma=False
        )
        return mapped(hidden, value, down, up, chosen, live)

    return run
```
